32 devices in a mesh: fsdp: 8 (over z, y), dp: 4 (over x, core).
Axes of the slice: x: 2, y: 2, z: 4, core: 2. Of those that a mesh axis runs over, the one named last changes fastest.
Arguments:
- glu_input: bfloat16 [8192, 3072], P(('fsdp', 'dp')), may hold values from -6 to 6
- frame_counts: int32 [32, 8], P(('fsdp', 'dp')), may hold values from 1 to 128, as said below
- send_rows: int32 [32, 256], P(('fsdp', 'dp')), may hold values from 0 to 256, as said below
- owner_rows: int32 [32, 160], P(('fsdp', 'dp')), may hold values from 0 to 255, as said below
- depth_kernel: float32 [5, 1536], replicated, may hold values from -2.5 to 2.5
- norm_gain: float32 [1536], replicated, may hold values from 0.25 to 1.75
- norm_bias: float32 [1536], replicated, may hold values from -3 to 3
- point_weight: bfloat16 [1536, 1536], P('fsdp'), may hold values from -0.15625 to 0.15625
- cotangent: bfloat16 [5120, 1536], P(('fsdp', 'dp')), may hold values from -6 to 6
Outputs:
- output: bfloat16 [5120, 1536], P(('fsdp', 'dp'))
- input_grad: bfloat16 [8192, 3072], P(('fsdp', 'dp'))
- kernel_grad: float32 [5, 1536], replicated
- norm_grad: float32 [2, 1536], replicated
The draws below stay inside these ranges and needn't reach their ends.
Inputs may be any that keep to these rules, and one draw needn't show every extreme that they name: `frame_counts`: A device's counts are the lengths of its 8 utterances. A device's total lies from 64 to 256, both reached at every dp index, and the totals of the devices with one dp index sum to 160 times the fsdp axis size. The longest utterance is reached at every dp index. `send_rows`: entry q of a device's list names the local slot whose activation goes to fsdp index q // 32 with the same dp index, as that owner's position q % 32 from this device; the value 256 marks an unused entry. Each live slot is named once, positions for one owner are used from the lowest up, and some device of every dp index fills all 32 positions for every owner. `owner_rows`: entry b names received position p: position p % 32 from fsdp index p // 32 of the same dp index. The 160 entries are distinct and are exactly the positions that senders use for this owner.
All inputs are finite; a program needn't handle non-finite values.
Results may differ from the reference program's by a relative error of at most 0.0085.
Values may be sent and summed in bfloat16 or wider, within the bound.
A program may use at most 64 MiB of HBM per device.

```python
import math
import jax
import jax.numpy as jnp
from jax import lax

CHANNELS = 1536
MODEL = 1536
KERNEL = 5
UTTS = 8
ROWS_DEV = 256
PEER_SLOTS = 32
OWNED = 160
ROWS = 8192
OWNED_ALL = 5120
N_FSDP = 8
N_DP = 4


def group_plan(key):
    devices = N_FSDP
    peer_slots = PEER_SLOTS
    owned_count = OWNED
    slot_count = ROWS_DEV
    base_share = owned_count // devices
    extra_owners = owned_count % devices
    pair_key, gain_key, row_key, owner_key, split_key = jax.random.split(key, 5)
    pair_order = jax.random.permutation(pair_key, devices)
    gainers = pair_order[0::2]
    losers = pair_order[1::2]
    surplus = jax.random.randint(gain_key, (devices // 2,), 0, slot_count - owned_count + 1)
    surplus = surplus.at[0].set(slot_count - owned_count)
    totals = jnp.zeros((devices,), jnp.int32).at[gainers].set(owned_count + surplus).at[losers].set(owned_count - surplus)
    source = jnp.arange(devices)[:, None]
    target = jnp.arange(devices)[None, :]
    base_count = base_share + ((target - source) % devices < extra_owners).astype(jnp.int32)
    offset = (target - gainers[:, None] - extra_owners) % devices
    wide_room = peer_slots - base_share
    room_left = jnp.where(offset < devices - extra_owners, wide_room, wide_room - 1)
    before = jnp.where(offset <= devices - extra_owners, offset * wide_room, (devices - extra_owners) * wide_room + (offset - devices + extra_owners) * (wide_room - 1))
    added = jnp.clip(surplus[:, None] - before, 0, room_left)
    counts = base_count.at[gainers].add(added).at[losers].add(-added)
    position = jnp.arange(slot_count)
    owner_of = position // peer_slots
    within = position % peer_slots
    live_send = within[None, :] < counts[:, owner_of]
    send_rank = jnp.clip(jnp.cumsum(live_send.astype(jnp.int32), axis=1) - 1, 0, slot_count - 1)

    def order_rows(sort_seed, total):
        shuffled = jax.random.permutation(sort_seed, slot_count)
        sort_keys = jnp.where(shuffled < total, position, slot_count + position)
        return shuffled[jnp.argsort(sort_keys, stable=True)]
    row_order = jax.vmap(order_rows)(jax.random.split(row_key, devices), totals)
    send_list = jnp.where(live_send, jnp.take_along_axis(row_order, send_rank, axis=1), slot_count)
    live_recv = within[None, :] < counts.T[:, owner_of]

    def order_slots(sort_seed, live_flags):
        shuffled = jax.random.permutation(sort_seed, slot_count)
        sort_keys = jnp.where(live_flags[shuffled], position, slot_count + position)
        return shuffled[jnp.argsort(sort_keys, stable=True)][:owned_count]
    owner_list = jax.vmap(order_slots)(jax.random.split(owner_key, devices), live_recv)
    weights = jax.random.randint(split_key, (devices, UTTS), 1, 6)
    cum_weight = jnp.cumsum(weights, axis=1)
    bounds = totals[:, None] * cum_weight // cum_weight[:, -1:]
    lengths = bounds - jnp.concatenate([jnp.zeros((devices, 1), bounds.dtype), bounds[:, :-1]], axis=1)
    first_full = gainers[0]
    half_rows = slot_count // 2
    rest_cum = jnp.cumsum(weights[first_full, 1:])
    rest_bounds = (slot_count - half_rows) * rest_cum // rest_cum[-1]
    rest_lengths = rest_bounds - jnp.concatenate([jnp.zeros((1,), rest_bounds.dtype), rest_bounds[:-1]])
    special = jnp.concatenate([jnp.full((1,), half_rows, rest_lengths.dtype), rest_lengths])
    lengths = lengths.at[first_full].set(special.astype(lengths.dtype))
    return (lengths, send_list, owner_list)


def full_plan(key):
    group_keys = jax.random.split(jax.random.fold_in(key, 11), N_DP)
    lengths, send_list, owner_list = jax.vmap(group_plan)(group_keys)

    def flatten(table):
        return jnp.swapaxes(table, 0, 1).reshape(N_FSDP * N_DP, table.shape[-1]).astype(jnp.int32)
    return (flatten(lengths), flatten(send_list), flatten(owner_list))


def draw_frame_counts(key, part):
    return full_plan(key)[0]


def draw_send_rows(key, part):
    return full_plan(key)[1]


def draw_owner_rows(key, part):
    return full_plan(key)[2]


def block_scale(key, extent, pieces, low, top_value):
    level, own = 1.0, jax.random.fold_in(key, 6)
    for dim, parts in pieces:
        steps = jnp.exp(jax.random.uniform(jax.random.fold_in(own, dim), (parts,), jnp.float32, low / len(pieces), top_value / len(pieces)))
        level = level * jnp.repeat(steps, extent[dim] // parts).reshape([-1 if axis == dim else 1 for axis in range(len(extent))])
    return level


def gaussian(key, extent, deviation, bound, cuts=(), kind=jnp.bfloat16):
    loudness = block_scale(key, extent, cuts, -0.22, 0.18) if cuts else 1.0
    array = jax.random.normal(key, extent, jnp.float32) * deviation * loudness
    return jnp.minimum(jnp.maximum(array, -bound), bound).astype(kind)


def setup_inputs(seed: int = 0) -> dict:
    keys = jax.random.split(jax.random.key(seed), 10)
    return {
        "glu_input": gaussian(keys[0], (ROWS, 2 * CHANNELS), 1.0, 6.0, ((0, 32),)),
        "frame_counts": draw_frame_counts(jax.random.fold_in(keys[9], 71), 0),
        "send_rows": draw_send_rows(jax.random.fold_in(keys[9], 71), 0),
        "owner_rows": draw_owner_rows(jax.random.fold_in(keys[9], 71), 0),
        "depth_kernel": gaussian(keys[4], (KERNEL, CHANNELS), KERNEL ** -0.5, 2.5, (), jnp.float32),
        "norm_gain": jnp.clip(1.0 + 0.15 * jax.random.normal(keys[5], (CHANNELS,), jnp.float32), 0.25, 1.75),
        "norm_bias": gaussian(keys[6], (CHANNELS,), 0.5, 3.0, (), jnp.float32),
        "point_weight": gaussian(keys[7], (CHANNELS, MODEL), CHANNELS ** -0.5, 0.15625, ((0, 8),)),
        "cotangent": gaussian(keys[8], (OWNED_ALL, MODEL), 1.0, 6.0, ((0, 32),)),
    }


eps = 1e-05

def conv_module(glu_rows, counts, kernel, gain_vec, bias_vec):
    row_count = glu_rows.shape[0]
    chan_count = kernel.shape[1]
    half_width = kernel.shape[0] // 2
    values = glu_rows.astype(jnp.float32)
    mixed_vals = values[:, :chan_count] * jax.nn.sigmoid(values[:, chan_count:])
    utter_ends = jnp.cumsum(counts.astype(jnp.int32))
    position = jnp.arange(row_count, dtype=jnp.int32)
    segment = lax.optimization_barrier(jnp.sum((position[:, None] >= utter_ends[None, :]).astype(jnp.int32), axis=1))
    is_live = position < utter_ends[-1]
    mixed_vals = jnp.where(is_live[:, None], mixed_vals, 0.0)
    padded = jnp.pad(mixed_vals, ((half_width, half_width), (0, 0)))
    labels = jnp.pad(segment, (half_width, half_width), constant_values=-1)
    conv_out = jnp.zeros((row_count, chan_count), jnp.float32)
    for offset in range(2 * half_width + 1):
        same_utt = labels[offset:offset + row_count] == segment
        conv_out = conv_out + jnp.where(same_utt[:, None], padded[offset:offset + row_count], 0.0) * kernel[offset]
    center = lax.optimization_barrier(jnp.mean(conv_out, axis=1, keepdims=True))
    spread = lax.optimization_barrier(jnp.mean(jnp.square(conv_out - center), axis=1, keepdims=True))
    normed = (conv_out - center) * lax.rsqrt(spread + eps) * gain_vec + bias_vec
    activated = normed * jax.nn.sigmoid(normed)
    return jnp.where(is_live[:, None], activated, 0.0)

def reference(glu_input, frame_counts, send_rows, owner_rows, depth_kernel, norm_gain, norm_bias, point_weight, cotangent):
    block_count = N_FSDP * N_DP
    glu_blocks = glu_input.reshape(block_count, ROWS_DEV, 2 * CHANNELS)

    def forward_block(block_items):
        return conv_module(block_items[0], block_items[1], depth_kernel, norm_gain, norm_bias).astype(jnp.bfloat16)
    activations = lax.map(forward_block, (glu_blocks, frame_counts)).reshape(block_count * ROWS_DEV, CHANNELS)
    owner_block = jnp.arange(block_count, dtype=jnp.int32)
    fsdp_index = owner_block // N_DP
    dp_index = owner_block % N_DP
    received_at = owner_rows.astype(jnp.int32)
    source_block = received_at // PEER_SLOTS * N_DP + dp_index[:, None]
    send_entry = fsdp_index[:, None] * PEER_SLOTS + received_at % PEER_SLOTS
    local_row = send_rows[source_block, send_entry].astype(jnp.int32)
    source_row = (source_block * ROWS_DEV + local_row).reshape(-1)
    owned_rows = activations[source_row]
    output = jnp.dot(owned_rows, point_weight, preferred_element_type=jnp.float32).astype(jnp.bfloat16)
    back_rows = jnp.dot(cotangent, point_weight.T, preferred_element_type=jnp.float32).astype(jnp.bfloat16)
    returned = jnp.zeros((block_count * ROWS_DEV, CHANNELS), jnp.bfloat16).at[source_row].set(back_rows)

    def backward_block(block_items):
        glu_block, counts, grad_block = block_items

        def local_pass(glu_rows, kernel, gain_vec, bias_vec):
            return conv_module(glu_rows, counts, kernel, gain_vec, bias_vec)
        unused, pullback = jax.vjp(local_pass, glu_block, depth_kernel, norm_gain, norm_bias)
        return pullback(grad_block.astype(jnp.float32))
    grad_parts = lax.map(backward_block, (glu_blocks, frame_counts, returned.reshape(block_count, ROWS_DEV, CHANNELS)))
    input_grad = grad_parts[0].reshape(block_count * ROWS_DEV, 2 * CHANNELS)
    grad_scale = 1.0 / math.sqrt(OWNED_ALL)
    kernel_grad = lax.optimization_barrier(jnp.sum(grad_parts[1], axis=0)) * grad_scale
    norm_grad = jnp.stack([lax.optimization_barrier(jnp.sum(grad_parts[2], axis=0)), lax.optimization_barrier(jnp.sum(grad_parts[3], axis=0))]) * grad_scale
    return (output, input_grad, kernel_grad, norm_grad)
```

```python
import functools
import math

import jax
import jax.numpy as jnp
from jax import lax
from jax.experimental import pallas as pl
from jax.experimental.pallas import tpu as pltpu
from jax.sharding import PartitionSpec as P

eps = 1e-05
LANES = 128
F32 = jnp.float32
BF16 = jnp.bfloat16


def fused_kernel(
    n_fsdp,
    n_dp,
    counts_ref,
    glu_ref,
    send_ref,
    owner_ref,
    taps_ref,
    gain_ref,
    bias_ref,
    weight_ref,
    cot_ref,
    out_ref,
    igrad_ref,
    kgrad_ref,
    ngrad_ref,
    w_buf,
    parked,
    returned,
    home,
    acts,
    outgoing,
    arrived,
    mixed_buf,
    conv_buf,
    grad_buf,
    back_buf,
    dp_in,
    rs_src,
    rs_in,
    full,
    w_send,
    w_recv,
    cot_send,
    cot_recv,
    act_send,
    act_recv,
    dp_send,
    dp_recv,
    rs_send,
    rs_recv,
    ag_send,
    ag_recv,
):
    f = lax.axis_index("fsdp")
    d = lax.axis_index("dp")
    rows = glu_ref.shape[0]
    chans = taps_ref.shape[1]
    taps = taps_ref.shape[0]
    half = taps // 2
    panel = weight_ref.shape[0]
    cols = weight_ref.shape[1]
    piece = cols // n_dp
    slots = rows // n_fsdp
    owned = cot_ref.shape[0]
    utts = counts_ref.shape[1]
    chunk = full.shape[1] // n_fsdp
    n_chunks = chans // LANES

    y_peer = f + 1 - 2 * (f % 2)
    x_peer = (d + n_dp // 2) % n_dp
    core_peer = d + 1 - 2 * (d % 2)

    barrier = pltpu.get_barrier_semaphore()
    for k in range(1, n_fsdp):
        pl.semaphore_signal(barrier, inc=1, device_id={"fsdp": (f + k) % n_fsdp, "dp": d})
    for k in range(1, n_dp):
        pl.semaphore_signal(barrier, inc=1, device_id={"fsdp": f, "dp": (d + k) % n_dp})
    pl.semaphore_wait(barrier, n_fsdp + n_dp - 2)

    def rows_of(p, size):
        return pl.ds(pl.multiple_of(p * size, size), size)

    def piece_of(p, q):
        return w_buf.at[rows_of(p, panel), rows_of(q, piece)]

    pending = []

    def send_piece(src, p, q, kind, slot, target):
        copy = pltpu.make_async_remote_copy(
            src_ref=src,
            dst_ref=piece_of(p, q),
            send_sem=w_send.at[kind, slot],
            recv_sem=w_recv.at[p, q],
            device_id=target,
        )
        copy.start()
        pending.append(copy)

    def wait_piece(p, q):
        pltpu.make_async_remote_copy(
            src_ref=piece_of(p, q),
            dst_ref=piece_of(p, q),
            send_sem=w_send.at[0, 0],
            recv_sem=w_recv.at[p, q],
            device_id={"fsdp": f, "dp": core_peer},
        ).wait_recv()

    own_piece = weight_ref.at[:, rows_of(d, piece)]
    z_steps = range(1, n_fsdp // 2)
    for k in z_steps:
        send_piece(own_piece, f, d, 0, k, {"fsdp": (f + 2 * k) % n_fsdp, "dp": d})
    send_piece(own_piece, f, d, 1, 0, {"fsdp": y_peer, "dp": d})

    def exchange(src, dst, send_sem, recv_sem):
        copies = []
        for k in range(1, n_fsdp):
            target = (f + k) % n_fsdp
            copy = pltpu.make_async_remote_copy(
                src_ref=src.at[rows_of(target, slots)],
                dst_ref=dst.at[rows_of(f, slots)],
                send_sem=send_sem.at[target],
                recv_sem=recv_sem.at[f],
                device_id={"fsdp": target, "dp": d},
            )
            copy.start()
            copies.append(copy)
        dst[rows_of(f, slots), :] = src[rows_of(f, slots), :]
        return copies

    def finish_exchange(copies, src, dst, send_sem, recv_sem):
        for k in range(1, n_fsdp):
            source = (f + k) % n_fsdp
            pltpu.make_async_remote_copy(
                src_ref=src.at[rows_of(source, slots)],
                dst_ref=dst.at[rows_of(source, slots)],
                send_sem=send_sem.at[source],
                recv_sem=recv_sem.at[source],
                device_id={"fsdp": source, "dp": d},
            ).wait_recv()
        pending.extend(copies)

    park = (
        lax.broadcasted_iota(jnp.int32, (rows, owned), 0) == owner_ref[...]
    ).astype(F32).astype(BF16)
    parked[...] = jnp.dot(park, cot_ref[...], preferred_element_type=F32).astype(BF16)
    cot_copies = exchange(parked, returned, cot_send, cot_recv)

    w_buf[rows_of(f, panel), :] = weight_ref[...]

    ends = []
    total = jnp.int32(0)
    for u in range(utts):
        total = total + counts_ref[0, u]
        ends.append(total)
    pos = lax.broadcasted_iota(jnp.int32, (rows, LANES), 0)

    def segment(at):
        seg = jnp.zeros((rows, LANES), jnp.int32)
        for end in ends:
            seg = seg + (at >= end).astype(jnp.int32)
        return seg

    own_seg = segment(pos)
    live = pos < total
    live_f = live.astype(F32)
    masks = []
    for j in range(taps):
        at = pos + (j - half)
        same = (segment(at) == own_seg) & live & (at >= 0) & (at < rows)
        masks.append(same.astype(F32))

    def lanes_of(i):
        return pl.ds(pl.multiple_of(i * LANES, LANES), LANES)

    def shifted(x, offset):
        return x if offset == 0 else pltpu.roll(x, (-offset) % rows, 0)

    def conv_step(i, acc):
        a = glu_ref[:, lanes_of(i)].astype(F32)
        b = glu_ref[:, pl.ds(pl.multiple_of(chans + i * LANES, LANES), LANES)].astype(F32)
        mixed = a * jax.nn.sigmoid(b) * live_f
        mixed_buf[:, lanes_of(i)] = mixed
        conv = jnp.zeros((rows, LANES), F32)
        for j in range(taps):
            conv = conv + masks[j] * shifted(mixed, j - half) * taps_ref[j : j + 1, lanes_of(i)]
        conv_buf[:, lanes_of(i)] = conv
        return acc + conv

    zero_acc = jnp.zeros((rows, LANES), F32)
    acc = lax.fori_loop(0, n_chunks, conv_step, zero_acc)
    mean = jnp.sum(acc, axis=1, keepdims=True) * (1.0 / chans)

    for k in z_steps:
        p = (f + 2 * k) % n_fsdp
        wait_piece(p, d)
        src = piece_of(p, d)
        send_piece(src, p, d, 1, k, {"fsdp": y_peer, "dp": d})
        send_piece(src, p, d, 2, k, {"fsdp": f, "dp": x_peer})
        send_piece(src, p, d, 3, k, {"fsdp": f, "dp": core_peer})

    def var_step(i, acc):
        diff = conv_buf[:, lanes_of(i)] - mean
        return acc + diff * diff

    acc = lax.fori_loop(0, n_chunks, var_step, zero_acc)
    rstd = lax.rsqrt(jnp.sum(acc, axis=1, keepdims=True) * (1.0 / chans) + eps)

    def act_step(i, carry):
        xhat = (conv_buf[:, lanes_of(i)] - mean) * rstd
        conv_buf[:, lanes_of(i)] = xhat
        normed = xhat * gain_ref[:, lanes_of(i)] + bias_ref[:, lanes_of(i)]
        acts[:, lanes_of(i)] = (normed * jax.nn.sigmoid(normed) * live_f).astype(BF16)
        return carry

    lax.fori_loop(0, n_chunks, act_step, 0)
    pick = (
        lax.broadcasted_iota(jnp.int32, (rows, rows), 0) == send_ref[...]
    ).astype(F32).astype(BF16)
    outgoing[...] = lax.dot_general(
        pick, acts[...], (((0,), (0,)), ((), ())), preferred_element_type=F32
    ).astype(BF16)

    for k in range(n_fsdp // 2):
        p = (y_peer + 2 * k) % n_fsdp
        wait_piece(p, d)
        src = piece_of(p, d)
        send_piece(src, p, d, 2, n_fsdp // 2 + k, {"fsdp": f, "dp": x_peer})
        send_piece(src, p, d, 3, n_fsdp // 2 + k, {"fsdp": f, "dp": core_peer})

    act_copies = exchange(outgoing, arrived, act_send, act_recv)

    order = [(f + 2 * k) % n_fsdp for k in z_steps]
    order += [(y_peer + 2 * k) % n_fsdp for k in range(n_fsdp // 2)]
    for k, p in enumerate(order):
        wait_piece(p, x_peer)
        send_piece(piece_of(p, x_peer), p, x_peer, 4, k, {"fsdp": f, "dp": core_peer})

    finish_exchange(cot_copies, parked, returned, cot_send, cot_recv)
    home[...] = jnp.dot(pick, returned[...], preferred_element_type=F32).astype(BF16)

    for p in order:
        wait_piece(p, core_peer)
        wait_piece(p, (core_peer + n_dp // 2) % n_dp)

    wide = 2 * LANES

    def back_step(i, carry):
        at = pl.ds(pl.multiple_of(i * wide, wide), wide)
        back_buf[:, at] = lax.dot_general(
            home[...], w_buf[at, :], (((1,), (1,)), ((), ())), preferred_element_type=F32
        ).astype(BF16)
        return carry

    lax.fori_loop(0, chans // wide, back_step, 0)

    part = dp_in.at[d]
    dp_in[d] = jnp.zeros(dp_in.shape[1:], F32)

    def norm_step(i, sums):
        xhat = conv_buf[:, lanes_of(i)]
        gain = gain_ref[:, lanes_of(i)]
        normed = xhat * gain + bias_ref[:, lanes_of(i)]
        s = jax.nn.sigmoid(normed)
        g = back_buf[:, lanes_of(i)].astype(F32) * live_f
        dn = g * (s + normed * s * (1.0 - s))
        dnx = dn * xhat
        part[taps : taps + 1, lanes_of(i)] = jnp.sum(dnx, axis=0, keepdims=True)
        part[taps + 1 : taps + 2, lanes_of(i)] = jnp.sum(dn, axis=0, keepdims=True)
        grad_buf[:, lanes_of(i)] = dn * gain
        return sums[0] + dn * gain, sums[1] + dnx * gain

    first, second = lax.fori_loop(0, n_chunks, norm_step, (zero_acc, zero_acc))
    first = jnp.sum(first, axis=1, keepdims=True) * (1.0 / chans)
    second = jnp.sum(second, axis=1, keepdims=True) * (1.0 / chans)

    def grad_step(i, carry):
        dconv = rstd * (grad_buf[:, lanes_of(i)] - first - conv_buf[:, lanes_of(i)] * second)
        mixed = mixed_buf[:, lanes_of(i)]
        dmixed = jnp.zeros((rows, LANES), F32)
        for j in range(taps):
            moved = masks[taps - 1 - j] * shifted(dconv, half - j)
            part[j : j + 1, lanes_of(i)] = jnp.sum(mixed * moved, axis=0, keepdims=True)
            dmixed = dmixed + moved * taps_ref[j : j + 1, lanes_of(i)]
        a = glu_ref[:, lanes_of(i)].astype(F32)
        right = pl.ds(pl.multiple_of(chans + i * LANES, LANES), LANES)
        sb = jax.nn.sigmoid(glu_ref[:, right].astype(F32))
        ds = dmixed * sb
        igrad_ref[:, lanes_of(i)] = ds.astype(BF16)
        igrad_ref[:, right] = (ds * a * (1.0 - sb)).astype(BF16)
        return carry

    lax.fori_loop(0, n_chunks, grad_step, 0)

    dp_copies = []
    for k in range(1, n_dp):
        target = (d + k) % n_dp
        copy = pltpu.make_async_remote_copy(
            src_ref=dp_in.at[d],
            dst_ref=dp_in.at[d],
            send_sem=dp_send.at[k],
            recv_sem=dp_recv.at[d],
            device_id={"fsdp": f, "dp": target},
        )
        copy.start()
        dp_copies.append(copy)

    finish_exchange(act_copies, outgoing, arrived, act_send, act_recv)
    outgoing_rows = lax.dot_general(
        park, arrived[...], (((0,), (0,)), ((), ())), preferred_element_type=F32
    ).astype(BF16)
    acts[0:owned, :] = outgoing_rows

    for k in range(1, n_dp):
        source = (d + k) % n_dp
        pltpu.make_async_remote_copy(
            src_ref=dp_in.at[source],
            dst_ref=dp_in.at[source],
            send_sem=dp_send.at[k],
            recv_sem=dp_recv.at[source],
            device_id={"fsdp": f, "dp": source},
        ).wait_recv()
    pending.extend(dp_copies)
    summed = dp_in[0]
    for q in range(1, n_dp):
        summed = summed + dp_in[q]
    rs_src[...] = summed

    rs_copies = []
    for k in range(1, n_fsdp):
        target = (f + k) % n_fsdp
        copy = pltpu.make_async_remote_copy(
            src_ref=rs_src.at[:, rows_of(target, chunk)],
            dst_ref=rs_in.at[f],
            send_sem=rs_send.at[target],
            recv_sem=rs_recv.at[f],
            device_id={"fsdp": target, "dp": d},
        )
        copy.start()
        rs_copies.append(copy)
    rs_in[f] = rs_src[:, rows_of(f, chunk)]

    def out_step(i, carry):
        at = pl.ds(pl.multiple_of(i * wide, wide), wide)
        out_ref[:, at] = jnp.dot(
            acts[0:owned, :], w_buf[:, at], preferred_element_type=F32
        ).astype(BF16)
        return carry

    lax.fori_loop(0, cols // wide, out_step, 0)

    for k in range(1, n_fsdp):
        source = (f + k) % n_fsdp
        pltpu.make_async_remote_copy(
            src_ref=rs_src.at[:, rows_of(source, chunk)],
            dst_ref=rs_in.at[source],
            send_sem=rs_send.at[source],
            recv_sem=rs_recv.at[source],
            device_id={"fsdp": source, "dp": d},
        ).wait_recv()
    pending.extend(rs_copies)
    reduced = rs_in[0]
    for q in range(1, n_fsdp):
        reduced = reduced + rs_in[q]
    scale = 1.0 / math.sqrt(owned * n_fsdp * n_dp)
    full[:, rows_of(f, chunk)] = reduced * scale
    ag_copies = []
    for k in range(1, n_fsdp):
        target = (f + k) % n_fsdp
        copy = pltpu.make_async_remote_copy(
            src_ref=full.at[:, rows_of(f, chunk)],
            dst_ref=full.at[:, rows_of(f, chunk)],
            send_sem=ag_send.at[target],
            recv_sem=ag_recv.at[f],
            device_id={"fsdp": target, "dp": d},
        )
        copy.start()
        ag_copies.append(copy)
    for k in range(1, n_fsdp):
        source = (f + k) % n_fsdp
        pltpu.make_async_remote_copy(
            src_ref=full.at[:, rows_of(source, chunk)],
            dst_ref=full.at[:, rows_of(source, chunk)],
            send_sem=ag_send.at[source],
            recv_sem=ag_recv.at[source],
            device_id={"fsdp": source, "dp": d},
        ).wait_recv()
    pending.extend(ag_copies)
    kgrad_ref[...] = full[0:taps, 0:chans]
    ngrad_ref[...] = full[taps : taps + 2, 0:chans]
    for copy in pending:
        copy.wait_send()


def fused_call(
    n_fsdp,
    n_dp,
    glu_input,
    frame_counts,
    send_rows,
    owner_rows,
    depth_kernel,
    norm_gain,
    norm_bias,
    point_weight,
    cotangent,
):
    rows, glu_cols = glu_input.shape
    taps, chans = depth_kernel.shape
    panel, cols = point_weight.shape
    owned = cotangent.shape[0]
    sum_rows = -(-(taps + 2) // 8) * 8
    chunk = -(-chans // (n_fsdp * LANES)) * LANES
    padded = chunk * n_fsdp
    vmem = pl.BlockSpec(memory_space=pltpu.VMEM)
    smem = pl.BlockSpec(memory_space=pltpu.SMEM)
    dma = pltpu.SemaphoreType.DMA
    return pl.pallas_call(
        functools.partial(fused_kernel, n_fsdp, n_dp),
        out_shape=(
            jax.ShapeDtypeStruct((owned, cols), BF16),
            jax.ShapeDtypeStruct((rows, glu_cols), BF16),
            jax.ShapeDtypeStruct((taps, chans), F32),
            jax.ShapeDtypeStruct((2, chans), F32),
        ),
        in_specs=[smem] + [vmem] * 8,
        out_specs=(vmem,) * 4,
        scratch_shapes=[
            pltpu.VMEM((chans, cols), BF16),
            pltpu.VMEM((rows, cols), BF16),
            pltpu.VMEM((rows, cols), BF16),
            pltpu.VMEM((rows, cols), BF16),
            pltpu.VMEM((rows, chans), BF16),
            pltpu.VMEM((rows, chans), BF16),
            pltpu.VMEM((rows, chans), BF16),
            pltpu.VMEM((rows, chans), F32),
            pltpu.VMEM((rows, chans), F32),
            pltpu.VMEM((rows, chans), F32),
            pltpu.VMEM((rows, chans), BF16),
            pltpu.VMEM((n_dp, sum_rows, padded), F32),
            pltpu.VMEM((sum_rows, padded), F32),
            pltpu.VMEM((n_fsdp, sum_rows, chunk), F32),
            pltpu.VMEM((sum_rows, padded), F32),
            dma((5, n_fsdp)),
            dma((n_fsdp, n_dp)),
            dma((n_fsdp,)),
            dma((n_fsdp,)),
            dma((n_fsdp,)),
            dma((n_fsdp,)),
            dma((n_dp,)),
            dma((n_dp,)),
            dma((n_fsdp,)),
            dma((n_fsdp,)),
            dma((n_fsdp,)),
            dma((n_fsdp,)),
        ],
        compiler_params=pltpu.CompilerParams(
            collective_id=0, has_side_effects=True, vmem_limit_bytes=56 * 1024 * 1024
        ),
        name="fused_module",
    )(
        frame_counts,
        glu_input,
        send_rows,
        owner_rows,
        depth_kernel,
        norm_gain.reshape(1, chans),
        norm_bias.reshape(1, chans),
        point_weight,
        cotangent,
    )


def conv_module(glu_rows, counts, kernel, gain_vec, bias_vec):
    row_count = glu_rows.shape[0]
    chan_count = kernel.shape[1]
    half_width = kernel.shape[0] // 2
    values = glu_rows.astype(jnp.float32)
    mixed_vals = values[:, :chan_count] * jax.nn.sigmoid(values[:, chan_count:])
    utter_ends = jnp.cumsum(counts)
    position = jnp.arange(row_count, dtype=jnp.int32)
    segment = jnp.sum((position[:, None] >= utter_ends[None, :]).astype(jnp.int32), axis=1)
    is_live = position < utter_ends[-1]
    mixed_vals = jnp.where(is_live[:, None], mixed_vals, 0.0)
    padded = jnp.pad(mixed_vals, ((half_width, half_width), (0, 0)))
    labels = jnp.pad(segment, (half_width, half_width), constant_values=-1)
    conv_out = jnp.zeros((row_count, chan_count), jnp.float32)
    for offset in range(2 * half_width + 1):
        same_utt = labels[offset : offset + row_count] == segment
        conv_out = (
            conv_out
            + jnp.where(same_utt[:, None], padded[offset : offset + row_count], 0.0)
            * kernel[offset]
        )
    center = jnp.mean(conv_out, axis=1, keepdims=True)
    spread = jnp.mean(jnp.square(conv_out - center), axis=1, keepdims=True)
    normed = (conv_out - center) * lax.rsqrt(spread + eps) * gain_vec + bias_vec
    activated = normed * jax.nn.sigmoid(normed)
    return jnp.where(is_live[:, None], activated, 0.0)


def per_device(
    glu_input,
    frame_counts,
    send_rows,
    owner_rows,
    depth_kernel,
    norm_gain,
    norm_bias,
    point_weight,
    cotangent,
):
    counts = frame_counts[0]
    send_slot = send_rows[0]
    owner_slot = owner_rows[0]
    row_count = glu_input.shape[0]
    out_count = point_weight.shape[1]

    def local_pass(glu_rows, kernel, gain_vec, bias_vec):
        return conv_module(glu_rows, counts, kernel, gain_vec, bias_vec)

    activated, pullback = jax.vjp(local_pass, glu_input, depth_kernel, norm_gain, norm_bias)
    activations = activated.astype(jnp.bfloat16)
    produced = jnp.dot(
        activations,
        lax.all_gather(point_weight, "fsdp", axis=0, tiled=True),
        preferred_element_type=jnp.float32,
    ).astype(jnp.bfloat16)
    outgoing = jnp.concatenate([produced, jnp.zeros((1, out_count), jnp.bfloat16)], axis=0)[
        send_slot
    ]
    arrived = lax.all_to_all(outgoing, "fsdp", split_axis=0, concat_axis=0, tiled=True)
    output = arrived[owner_slot]
    parked = jnp.zeros((row_count, out_count), jnp.bfloat16).at[owner_slot].set(cotangent)
    returned = lax.all_to_all(parked, "fsdp", split_axis=0, concat_axis=0, tiled=True)
    home_rows = (
        jnp.zeros((row_count + 1, out_count), jnp.bfloat16).at[send_slot].set(returned)[:row_count]
    )
    grad_acts = lax.dot_general(
        home_rows,
        lax.all_gather(point_weight, "fsdp", axis=0, tiled=True),
        (((1,), (1,)), ((), ())),
        preferred_element_type=jnp.float32,
    ).astype(jnp.bfloat16)
    input_grad, kernel_part, gain_part, bias_part = pullback(grad_acts.astype(jnp.float32))
    totals = lax.psum((kernel_part, jnp.stack([gain_part, bias_part])), ("fsdp", "dp"))
    frame_total = owner_slot.shape[0] * lax.axis_size("fsdp") * lax.axis_size("dp")
    grad_scale = 1.0 / math.sqrt(frame_total)
    return (output, input_grad, totals[0] * grad_scale, totals[1] * grad_scale)


def solution(mesh):
    in_specs = (
        P(("fsdp", "dp"), None),
        P(("fsdp", "dp"), None),
        P(("fsdp", "dp"), None),
        P(("fsdp", "dp"), None),
        P(),
        P(),
        P(),
        P("fsdp", None),
        P(("fsdp", "dp"), None),
    )
    out_specs = (P(("fsdp", "dp"), None), P(("fsdp", "dp"), None), P(), P())
    n_fsdp, n_dp = mesh.shape["fsdp"], mesh.shape["dp"]

    def local(*args):
        slots = args[2].shape[1] // n_fsdp
        panel = args[7].shape[0]
        if slots % 16 == 0 and panel % 16 == 0 and n_fsdp % 2 == 0 and n_dp == 4:
            return fused_call(n_fsdp, n_dp, *args)
        return per_device(*args)

    return jax.shard_map(
        local, mesh=mesh, in_specs=in_specs, out_specs=out_specs, check_vma=False
    )
```

```python
import functools
import math

import jax
import jax.numpy as jnp
from jax import lax
from jax.experimental import pallas as pl
from jax.experimental.pallas import tpu as pltpu
from jax.sharding import PartitionSpec as P

eps = 1e-05
LANES = 128
COPY_PARTS = 2
F32 = jnp.float32
BF16 = jnp.bfloat16


def sigmoid(x):
    return 0.5 * jnp.tanh(0.5 * x) + 0.5


def copy_kernel(*refs):
    sources, targets, sems = refs[:4], refs[4:8], refs[8]
    copies = []
    for i, (source, target) in enumerate(zip(sources, targets)):
        size = source.shape[0]
        parts = COPY_PARTS if size % (16 * COPY_PARTS) == 0 else 1
        step = size // parts
        for k in range(parts):
            at = pl.ds(k * step, step)
            src, dst = (source, target) if parts == 1 else (source.at[at], target.at[at])
            copies.append(pltpu.make_async_copy(src, dst, sems.at[i, k]))
    for copy in copies:
        copy.start()
    for copy in copies:
        copy.wait()


def fused_kernel(
    n_fsdp,
    n_dp,
    counts_ref,
    glu_ref,
    send_ref,
    owner_ref,
    taps_ref,
    gain_ref,
    bias_ref,
    weight_ref,
    cot_ref,
    out_ref,
    igrad_ref,
    kgrad_ref,
    ngrad_ref,
    w_buf,
    parked,
    returned,
    home,
    acts,
    outgoing,
    arrived,
    mixed_buf,
    conv_buf,
    grad_buf,
    back_buf,
    dp_in,
    rs_src,
    rs_in,
    full,
    w_send,
    w_recv,
    cot_send,
    cot_recv,
    act_send,
    act_recv,
    dp_send,
    dp_recv,
    rs_send,
    rs_recv,
    ag_send,
    ag_recv,
):
    f = lax.axis_index("fsdp")
    d = lax.axis_index("dp")
    rows = glu_ref.shape[0]
    chans = taps_ref.shape[1]
    taps = taps_ref.shape[0]
    half = taps // 2
    panel = weight_ref.shape[0]
    cols = weight_ref.shape[1]
    piece = cols // n_dp
    slots = rows // n_fsdp
    owned = cot_ref.shape[0]
    utts = counts_ref.shape[1]
    chunk = full.shape[1] // n_fsdp
    n_chunks = chans // LANES

    y_peer = f + 1 - 2 * (f % 2)
    x_peer = (d + n_dp // 2) % n_dp
    core_peer = d + 1 - 2 * (d % 2)

    barrier = pltpu.get_barrier_semaphore()
    for k in range(1, n_fsdp):
        pl.semaphore_signal(barrier, inc=1, device_id={"fsdp": (f + k) % n_fsdp, "dp": d})
    for k in range(1, n_dp):
        pl.semaphore_signal(barrier, inc=1, device_id={"fsdp": f, "dp": (d + k) % n_dp})
    pl.semaphore_wait(barrier, n_fsdp + n_dp - 2)

    def rows_of(p, size):
        return pl.ds(pl.multiple_of(p * size, size), size)

    def piece_of(p, q):
        return w_buf.at[rows_of(p, panel), rows_of(q, piece)]

    pending = []

    def send_piece(src, p, q, kind, slot, target):
        copy = pltpu.make_async_remote_copy(
            src_ref=src,
            dst_ref=piece_of(p, q),
            send_sem=w_send.at[kind, slot],
            recv_sem=w_recv.at[p, q],
            device_id=target,
        )
        copy.start()
        pending.append(copy)

    def wait_piece(p, q):
        pltpu.make_async_remote_copy(
            src_ref=piece_of(p, q),
            dst_ref=piece_of(p, q),
            send_sem=w_send.at[0, 0],
            recv_sem=w_recv.at[p, q],
            device_id={"fsdp": f, "dp": core_peer},
        ).wait_recv()

    own_piece = weight_ref.at[:, rows_of(d, piece)]
    z_steps = range(1, n_fsdp // 2)
    for k in z_steps:
        send_piece(own_piece, f, d, 0, k, {"fsdp": (f + 2 * k) % n_fsdp, "dp": d})
    send_piece(own_piece, f, d, 1, 0, {"fsdp": y_peer, "dp": d})

    def exchange(src, dst, send_sem, recv_sem):
        copies = []
        for k in range(1, n_fsdp):
            target = (f + k) % n_fsdp
            copy = pltpu.make_async_remote_copy(
                src_ref=src.at[rows_of(target, slots)],
                dst_ref=dst.at[rows_of(f, slots)],
                send_sem=send_sem.at[target],
                recv_sem=recv_sem.at[f],
                device_id={"fsdp": target, "dp": d},
            )
            copy.start()
            copies.append(copy)
        dst[rows_of(f, slots), :] = src[rows_of(f, slots), :]
        return copies

    def finish_exchange(copies, src, dst, send_sem, recv_sem):
        for k in range(1, n_fsdp):
            source = (f + k) % n_fsdp
            pltpu.make_async_remote_copy(
                src_ref=src.at[rows_of(source, slots)],
                dst_ref=dst.at[rows_of(source, slots)],
                send_sem=send_sem.at[source],
                recv_sem=recv_sem.at[source],
                device_id={"fsdp": source, "dp": d},
            ).wait_recv()
        pending.extend(copies)

    park = (
        lax.broadcasted_iota(jnp.int32, (rows, owned), 0) == owner_ref[...]
    ).astype(F32).astype(BF16)
    parked[...] = jnp.dot(park, cot_ref[...], preferred_element_type=F32).astype(BF16)

    w_buf[rows_of(f, panel), :] = weight_ref[...]

    ends = []
    total = jnp.int32(0)
    for u in range(utts):
        total = total + counts_ref[0, u]
        ends.append(total)
    pos = lax.broadcasted_iota(jnp.int32, (rows, LANES), 0)

    def segment(at):
        seg = jnp.zeros((rows, LANES), jnp.int32)
        for end in ends:
            seg = seg + (at >= end).astype(jnp.int32)
        return seg

    own_seg = segment(pos)
    live = pos < total
    live_f = live.astype(F32)
    masks = []
    for j in range(taps):
        at = pos + (j - half)
        same = (segment(at) == own_seg) & live & (at >= 0) & (at < rows)
        masks.append(same.astype(F32))

    def lanes_of(i):
        return pl.ds(pl.multiple_of(i * LANES, LANES), LANES)

    def shifted(x, offset):
        return x if offset == 0 else pltpu.roll(x, (-offset) % rows, 0)

    def conv_step(i, acc):
        a = glu_ref[:, lanes_of(i)].astype(F32)
        b = glu_ref[:, pl.ds(pl.multiple_of(chans + i * LANES, LANES), LANES)].astype(F32)
        mixed = a * sigmoid(b) * live_f
        mixed_buf[:, lanes_of(i)] = mixed
        conv = jnp.zeros((rows, LANES), F32)
        for j in range(taps):
            conv = conv + masks[j] * shifted(mixed, j - half) * taps_ref[j : j + 1, lanes_of(i)]
        conv_buf[:, lanes_of(i)] = conv
        return acc + conv

    zero_acc = jnp.zeros((rows, LANES), F32)
    def forward_y(k):
        p = (y_peer + 2 * k) % n_fsdp
        wait_piece(p, d)
        src = piece_of(p, d)
        send_piece(src, p, d, 2, n_fsdp // 2 + k, {"fsdp": f, "dp": x_peer})
        send_piece(src, p, d, 3, n_fsdp // 2 + k, {"fsdp": f, "dp": core_peer})

    acc = lax.fori_loop(0, n_chunks // 2, conv_step, zero_acc)
    forward_y(0)
    acc = lax.fori_loop(n_chunks // 2, n_chunks, conv_step, acc)
    mean = jnp.sum(acc, axis=1, keepdims=True) * (1.0 / chans)

    for k in z_steps:
        p = (f + 2 * k) % n_fsdp
        wait_piece(p, d)
        src = piece_of(p, d)
        send_piece(src, p, d, 1, k, {"fsdp": y_peer, "dp": d})
        send_piece(src, p, d, 2, k, {"fsdp": f, "dp": x_peer})
        send_piece(src, p, d, 3, k, {"fsdp": f, "dp": core_peer})

    cot_copies = exchange(parked, returned, cot_send, cot_recv)

    def var_step(i, acc):
        diff = conv_buf[:, lanes_of(i)] - mean
        return acc + diff * diff

    acc = lax.fori_loop(0, n_chunks, var_step, zero_acc)
    rstd = lax.rsqrt(jnp.sum(acc, axis=1, keepdims=True) * (1.0 / chans) + eps)

    def act_step(i, carry):
        xhat = (conv_buf[:, lanes_of(i)] - mean) * rstd
        conv_buf[:, lanes_of(i)] = xhat
        normed = xhat * gain_ref[lanes_of(i)][None, :] + bias_ref[lanes_of(i)][None, :]
        acts[:, lanes_of(i)] = (normed * sigmoid(normed) * live_f).astype(BF16)
        return carry

    lax.fori_loop(0, n_chunks, act_step, 0)
    pick = (
        lax.broadcasted_iota(jnp.int32, (rows, rows), 0) == send_ref[...]
    ).astype(F32).astype(BF16)
    outgoing[...] = lax.dot_general(
        pick, acts[...], (((0,), (0,)), ((), ())), preferred_element_type=F32
    ).astype(BF16)

    for k in z_steps:
        forward_y(k)

    order = [((y_peer + 2 * k) % n_fsdp, n_fsdp // 2 + k) for k in range(1)]
    order += [((f + 2 * k) % n_fsdp, k) for k in z_steps]
    order += [((y_peer + 2 * k) % n_fsdp, n_fsdp // 2 + k) for k in z_steps]
    for p, k in order:
        wait_piece(p, x_peer)
        send_piece(piece_of(p, x_peer), p, x_peer, 4, k, {"fsdp": f, "dp": core_peer})

    finish_exchange(cot_copies, parked, returned, cot_send, cot_recv)
    act_copies = exchange(outgoing, arrived, act_send, act_recv)
    home[...] = jnp.dot(pick, returned[...], preferred_element_type=F32).astype(BF16)

    wide = 2 * LANES

    for k in range(n_fsdp // 2):
        arrivals = [(y_peer + 2 * k) % n_fsdp]
        if k > 0:
            arrivals.append((f + 2 * k) % n_fsdp)
        for p in arrivals:
            wait_piece(p, core_peer)
            wait_piece(p, (core_peer + n_dp // 2) % n_dp)
        at = rows_of((f // 2 + k) % (n_fsdp // 2), 2 * panel)
        back_buf[:, at] = lax.dot_general(
            home[...], w_buf[at, :], (((1,), (1,)), ((), ())), preferred_element_type=F32
        ).astype(BF16)

    part = dp_in.at[d]
    dp_in[d] = jnp.zeros(dp_in.shape[1:], F32)

    def norm_step(i, sums):
        xhat = conv_buf[:, lanes_of(i)]
        gain = gain_ref[lanes_of(i)][None, :]
        normed = xhat * gain + bias_ref[lanes_of(i)][None, :]
        s = sigmoid(normed)
        g = back_buf[:, lanes_of(i)].astype(F32) * live_f
        dn = g * (s + normed * s * (1.0 - s))
        dnx = dn * xhat
        part[taps : taps + 1, lanes_of(i)] = jnp.sum(dnx, axis=0, keepdims=True)
        part[taps + 1 : taps + 2, lanes_of(i)] = jnp.sum(dn, axis=0, keepdims=True)
        grad_buf[:, lanes_of(i)] = dn * gain
        return sums[0] + dn * gain, sums[1] + dnx * gain

    first, second = lax.fori_loop(0, n_chunks, norm_step, (zero_acc, zero_acc))
    first = jnp.sum(first, axis=1, keepdims=True) * (1.0 / chans)
    second = jnp.sum(second, axis=1, keepdims=True) * (1.0 / chans)

    def grad_step(i, carry):
        dconv = rstd * (grad_buf[:, lanes_of(i)] - first - conv_buf[:, lanes_of(i)] * second)
        mixed = mixed_buf[:, lanes_of(i)]
        dmixed = jnp.zeros((rows, LANES), F32)
        for j in range(taps):
            moved = masks[taps - 1 - j] * shifted(dconv, half - j)
            part[j : j + 1, lanes_of(i)] = jnp.sum(mixed * moved, axis=0, keepdims=True)
            dmixed = dmixed + moved * taps_ref[j : j + 1, lanes_of(i)]
        grad_buf[:, lanes_of(i)] = dmixed
        return carry

    lax.fori_loop(0, n_chunks, grad_step, 0)

    dp_copies = []
    for k in range(1, n_dp):
        target = (d + k) % n_dp
        copy = pltpu.make_async_remote_copy(
            src_ref=dp_in.at[d],
            dst_ref=dp_in.at[d],
            send_sem=dp_send.at[k],
            recv_sem=dp_recv.at[d],
            device_id={"fsdp": f, "dp": target},
        )
        copy.start()
        dp_copies.append(copy)

    def input_step(i, carry):
        a = glu_ref[:, lanes_of(i)].astype(F32)
        right = pl.ds(pl.multiple_of(chans + i * LANES, LANES), LANES)
        sb = sigmoid(glu_ref[:, right].astype(F32))
        ds = grad_buf[:, lanes_of(i)] * sb
        igrad_ref[:, lanes_of(i)] = ds.astype(BF16)
        igrad_ref[:, right] = (ds * a * (1.0 - sb)).astype(BF16)
        return carry

    lax.fori_loop(0, n_chunks, input_step, 0)

    for k in range(1, n_dp):
        source = (d + k) % n_dp
        pltpu.make_async_remote_copy(
            src_ref=dp_in.at[source],
            dst_ref=dp_in.at[source],
            send_sem=dp_send.at[k],
            recv_sem=dp_recv.at[source],
            device_id={"fsdp": f, "dp": source},
        ).wait_recv()
    pending.extend(dp_copies)
    summed = dp_in[0]
    for q in range(1, n_dp):
        summed = summed + dp_in[q]
    rs_src[...] = summed

    rs_copies = []
    for k in range(1, n_fsdp):
        target = (f + k) % n_fsdp
        copy = pltpu.make_async_remote_copy(
            src_ref=rs_src.at[:, rows_of(target, chunk)],
            dst_ref=rs_in.at[f],
            send_sem=rs_send.at[target],
            recv_sem=rs_recv.at[f],
            device_id={"fsdp": target, "dp": d},
        )
        copy.start()
        rs_copies.append(copy)
    rs_in[f] = rs_src[:, rows_of(f, chunk)]

    finish_exchange(act_copies, outgoing, arrived, act_send, act_recv)
    outgoing_rows = lax.dot_general(
        park, arrived[...], (((0,), (0,)), ((), ())), preferred_element_type=F32
    ).astype(BF16)
    acts[0:owned, :] = outgoing_rows

    def out_step(i, carry):
        at = pl.ds(pl.multiple_of(i * wide, wide), wide)
        out_ref[:, at] = jnp.dot(
            acts[0:owned, :], w_buf[:, at], preferred_element_type=F32
        ).astype(BF16)
        return carry

    lax.fori_loop(0, cols // wide, out_step, 0)

    for k in range(1, n_fsdp):
        source = (f + k) % n_fsdp
        pltpu.make_async_remote_copy(
            src_ref=rs_src.at[:, rows_of(source, chunk)],
            dst_ref=rs_in.at[source],
            send_sem=rs_send.at[source],
            recv_sem=rs_recv.at[source],
            device_id={"fsdp": source, "dp": d},
        ).wait_recv()
    pending.extend(rs_copies)
    reduced = rs_in[0]
    for q in range(1, n_fsdp):
        reduced = reduced + rs_in[q]
    scale = 1.0 / math.sqrt(owned * n_fsdp * n_dp)
    full[:, rows_of(f, chunk)] = reduced * scale
    ag_copies = []
    for k in range(1, n_fsdp):
        target = (f + k) % n_fsdp
        copy = pltpu.make_async_remote_copy(
            src_ref=full.at[:, rows_of(f, chunk)],
            dst_ref=full.at[:, rows_of(f, chunk)],
            send_sem=ag_send.at[target],
            recv_sem=ag_recv.at[f],
            device_id={"fsdp": target, "dp": d},
        )
        copy.start()
        ag_copies.append(copy)
    for k in range(1, n_fsdp):
        source = (f + k) % n_fsdp
        pltpu.make_async_remote_copy(
            src_ref=full.at[:, rows_of(source, chunk)],
            dst_ref=full.at[:, rows_of(source, chunk)],
            send_sem=ag_send.at[source],
            recv_sem=ag_recv.at[source],
            device_id={"fsdp": source, "dp": d},
        ).wait_recv()
    pending.extend(ag_copies)
    kgrad_ref[...] = full[0:taps, 0:chans]
    ngrad_ref[...] = full[taps : taps + 2, 0:chans]
    for copy in pending:
        copy.wait_send()


def fused_call(
    n_fsdp,
    n_dp,
    glu_input,
    frame_counts,
    send_rows,
    owner_rows,
    depth_kernel,
    norm_gain,
    norm_bias,
    point_weight,
    cotangent,
):
    rows, glu_cols = glu_input.shape
    taps, chans = depth_kernel.shape
    panel, cols = point_weight.shape
    owned = cotangent.shape[0]
    sum_rows = -(-(taps + 2) // 8) * 8
    chunk = -(-chans // (n_fsdp * LANES)) * LANES
    padded = chunk * n_fsdp
    vmem = pl.BlockSpec(memory_space=pltpu.VMEM)
    smem = pl.BlockSpec(memory_space=pltpu.SMEM)
    dma = pltpu.SemaphoreType.DMA
    results = pl.pallas_call(
        functools.partial(fused_kernel, n_fsdp, n_dp),
        out_shape=(
            jax.ShapeDtypeStruct((owned, cols), BF16),
            jax.ShapeDtypeStruct((rows, glu_cols), BF16),
            jax.ShapeDtypeStruct((taps, chans), F32),
            jax.ShapeDtypeStruct((2, chans), F32),
        ),
        in_specs=[smem] + [vmem] * 8,
        out_specs=(vmem,) * 4,
        scratch_shapes=[
            pltpu.VMEM((chans, cols), BF16),
            pltpu.VMEM((rows, cols), BF16),
            pltpu.VMEM((rows, cols), BF16),
            pltpu.VMEM((rows, cols), BF16),
            pltpu.VMEM((rows, chans), BF16),
            pltpu.VMEM((rows, chans), BF16),
            pltpu.VMEM((rows, chans), BF16),
            pltpu.VMEM((rows, chans), F32),
            pltpu.VMEM((rows, chans), F32),
            pltpu.VMEM((rows, chans), F32),
            pltpu.VMEM((rows, chans), BF16),
            pltpu.VMEM((n_dp, sum_rows, padded), F32),
            pltpu.VMEM((sum_rows, padded), F32),
            pltpu.VMEM((n_fsdp, sum_rows, chunk), F32),
            pltpu.VMEM((sum_rows, padded), F32),
            dma((5, n_fsdp)),
            dma((n_fsdp, n_dp)),
            dma((n_fsdp,)),
            dma((n_fsdp,)),
            dma((n_fsdp,)),
            dma((n_fsdp,)),
            dma((n_dp,)),
            dma((n_dp,)),
            dma((n_fsdp,)),
            dma((n_fsdp,)),
            dma((n_fsdp,)),
            dma((n_fsdp,)),
        ],
        compiler_params=pltpu.CompilerParams(
            collective_id=0, has_side_effects=True, vmem_limit_bytes=56 * 1024 * 1024
        ),
        name="fused_module",
    )(
        frame_counts,
        glu_input,
        send_rows,
        owner_rows,
        depth_kernel,
        norm_gain,
        norm_bias,
        point_weight,
        cotangent,
    )
    anywhere = pl.BlockSpec(memory_space=pl.ANY)
    return tuple(
        pl.pallas_call(
            copy_kernel,
            out_shape=tuple(jax.ShapeDtypeStruct(r.shape, r.dtype) for r in results),
            in_specs=[anywhere] * 4,
            out_specs=(anywhere,) * 4,
            scratch_shapes=[dma((4, COPY_PARTS))],
            compiler_params=pltpu.CompilerParams(vmem_limit_bytes=60 * 1024 * 1024),
            name="copy_results",
        )(*results)
    )


def conv_module(glu_rows, counts, kernel, gain_vec, bias_vec):
    row_count = glu_rows.shape[0]
    chan_count = kernel.shape[1]
    half_width = kernel.shape[0] // 2
    values = glu_rows.astype(jnp.float32)
    mixed_vals = values[:, :chan_count] * jax.nn.sigmoid(values[:, chan_count:])
    utter_ends = jnp.cumsum(counts)
    position = jnp.arange(row_count, dtype=jnp.int32)
    segment = jnp.sum((position[:, None] >= utter_ends[None, :]).astype(jnp.int32), axis=1)
    is_live = position < utter_ends[-1]
    mixed_vals = jnp.where(is_live[:, None], mixed_vals, 0.0)
    padded = jnp.pad(mixed_vals, ((half_width, half_width), (0, 0)))
    labels = jnp.pad(segment, (half_width, half_width), constant_values=-1)
    conv_out = jnp.zeros((row_count, chan_count), jnp.float32)
    for offset in range(2 * half_width + 1):
        same_utt = labels[offset : offset + row_count] == segment
        conv_out = (
            conv_out
            + jnp.where(same_utt[:, None], padded[offset : offset + row_count], 0.0)
            * kernel[offset]
        )
    center = jnp.mean(conv_out, axis=1, keepdims=True)
    spread = jnp.mean(jnp.square(conv_out - center), axis=1, keepdims=True)
    normed = (conv_out - center) * lax.rsqrt(spread + eps) * gain_vec + bias_vec
    activated = normed * jax.nn.sigmoid(normed)
    return jnp.where(is_live[:, None], activated, 0.0)


def per_device(
    glu_input,
    frame_counts,
    send_rows,
    owner_rows,
    depth_kernel,
    norm_gain,
    norm_bias,
    point_weight,
    cotangent,
):
    counts = frame_counts[0]
    send_slot = send_rows[0]
    owner_slot = owner_rows[0]
    row_count = glu_input.shape[0]
    out_count = point_weight.shape[1]

    def local_pass(glu_rows, kernel, gain_vec, bias_vec):
        return conv_module(glu_rows, counts, kernel, gain_vec, bias_vec)

    activated, pullback = jax.vjp(local_pass, glu_input, depth_kernel, norm_gain, norm_bias)
    activations = activated.astype(jnp.bfloat16)
    produced = jnp.dot(
        activations,
        lax.all_gather(point_weight, "fsdp", axis=0, tiled=True),
        preferred_element_type=jnp.float32,
    ).astype(jnp.bfloat16)
    outgoing = jnp.concatenate([produced, jnp.zeros((1, out_count), jnp.bfloat16)], axis=0)[
        send_slot
    ]
    arrived = lax.all_to_all(outgoing, "fsdp", split_axis=0, concat_axis=0, tiled=True)
    output = arrived[owner_slot]
    parked = jnp.zeros((row_count, out_count), jnp.bfloat16).at[owner_slot].set(cotangent)
    returned = lax.all_to_all(parked, "fsdp", split_axis=0, concat_axis=0, tiled=True)
    home_rows = (
        jnp.zeros((row_count + 1, out_count), jnp.bfloat16).at[send_slot].set(returned)[:row_count]
    )
    grad_acts = lax.dot_general(
        home_rows,
        lax.all_gather(point_weight, "fsdp", axis=0, tiled=True),
        (((1,), (1,)), ((), ())),
        preferred_element_type=jnp.float32,
    ).astype(jnp.bfloat16)
    input_grad, kernel_part, gain_part, bias_part = pullback(grad_acts.astype(jnp.float32))
    totals = lax.psum((kernel_part, jnp.stack([gain_part, bias_part])), ("fsdp", "dp"))
    frame_total = owner_slot.shape[0] * lax.axis_size("fsdp") * lax.axis_size("dp")
    grad_scale = 1.0 / math.sqrt(frame_total)
    return (output, input_grad, totals[0] * grad_scale, totals[1] * grad_scale)


def solution(mesh):
    in_specs = (
        P(("fsdp", "dp"), None),
        P(("fsdp", "dp"), None),
        P(("fsdp", "dp"), None),
        P(("fsdp", "dp"), None),
        P(),
        P(),
        P(),
        P("fsdp", None),
        P(("fsdp", "dp"), None),
    )
    out_specs = (P(("fsdp", "dp"), None), P(("fsdp", "dp"), None), P(), P())
    n_fsdp, n_dp = mesh.shape["fsdp"], mesh.shape["dp"]

    def local(*args):
        slots = args[2].shape[1] // n_fsdp
        panel = args[7].shape[0]
        if slots % 16 == 0 and panel % 16 == 0 and n_fsdp % 2 == 0 and n_dp == 4 and panel % 64 == 0:
            return fused_call(n_fsdp, n_dp, *args)
        return per_device(*args)

    return jax.shard_map(
        local, mesh=mesh, in_specs=in_specs, out_specs=out_specs, check_vma=False
    )
```

```python
import functools
import math

import jax
import jax.numpy as jnp
from jax import lax
from jax.experimental import pallas as pl
from jax.experimental.pallas import tpu as pltpu
from jax.sharding import PartitionSpec as P

eps = 1e-05
LANES = 128
COPY_PARTS = 2
F32 = jnp.float32
BF16 = jnp.bfloat16


def sigmoid(x):
    return 0.5 * jnp.tanh(0.5 * x) + 0.5


def copy_kernel(*refs):
    sources, targets, stages, in_sems, out_sems = refs[:4], refs[4:8], refs[8:12], refs[12], refs[13]
    loads, stores = [], []
    for i, (source, target, stage) in enumerate(zip(sources, targets, stages)):
        size = source.shape[0]
        parts = COPY_PARTS if size % (16 * COPY_PARTS) == 0 else 1
        step = size // parts
        for k in range(parts):
            at = pl.ds(k * step, step)
            src, mid, dst = (r if parts == 1 else r.at[at] for r in (source, stage, target))
            loads.append(pltpu.make_async_copy(src, mid, in_sems.at[i, k]))
            stores.append(pltpu.make_async_copy(mid, dst, out_sems.at[i, k]))
    for load in loads:
        load.start()
    for load, store in zip(loads, stores):
        load.wait()
        store.start()
    for store in stores:
        store.wait()


def fused_kernel(
    n_fsdp,
    n_dp,
    counts_ref,
    glu_ref,
    send_ref,
    owner_ref,
    taps_ref,
    gain_ref,
    bias_ref,
    weight_ref,
    cot_ref,
    out_ref,
    igrad_ref,
    kgrad_ref,
    ngrad_ref,
    w_buf,
    parked,
    returned,
    home,
    acts,
    outgoing,
    arrived,
    mixed_buf,
    conv_buf,
    grad_buf,
    back_buf,
    dp_in,
    rs_src,
    rs_in,
    full,
    w_send,
    w_recv,
    cot_send,
    cot_recv,
    act_send,
    act_recv,
    dp_send,
    dp_recv,
    rs_send,
    rs_recv,
    ag_send,
    ag_recv,
):
    f = lax.axis_index("fsdp")
    d = lax.axis_index("dp")
    rows = glu_ref.shape[0]
    chans = taps_ref.shape[1]
    taps = taps_ref.shape[0]
    half = taps // 2
    panel = weight_ref.shape[0]
    cols = weight_ref.shape[1]
    piece = cols // n_dp
    slots = rows // n_fsdp
    owned = cot_ref.shape[0]
    utts = counts_ref.shape[1]
    chunk = full.shape[1] // n_fsdp
    n_chunks = chans // LANES

    y_peer = f + 1 - 2 * (f % 2)
    x_peer = (d + n_dp // 2) % n_dp
    core_peer = d + 1 - 2 * (d % 2)

    barrier = pltpu.get_barrier_semaphore()
    for k in range(1, n_fsdp):
        pl.semaphore_signal(barrier, inc=1, device_id={"fsdp": (f + k) % n_fsdp, "dp": d})
    for k in range(1, n_dp):
        pl.semaphore_signal(barrier, inc=1, device_id={"fsdp": f, "dp": (d + k) % n_dp})
    pl.semaphore_wait(barrier, n_fsdp + n_dp - 2)

    def rows_of(p, size):
        return pl.ds(pl.multiple_of(p * size, size), size)

    def piece_of(p, q):
        return w_buf.at[rows_of(p, panel), rows_of(q, piece)]

    pending = []
    zi = f // 2
    n_z = n_fsdp // 2
    up, down = {"fsdp": (f + 2) % n_fsdp, "dp": d}, {"fsdp": (f + n_fsdp - 2) % n_fsdp, "dp": d}
    to_y, to_x, to_core = (
        {"fsdp": y_peer, "dp": d},
        {"fsdp": f, "dp": x_peer},
        {"fsdp": f, "dp": core_peer},
    )
    can_up, can_down = zi + 1 < n_z, zi >= 1

    def piece_copy(src, p, q, kind, target):
        return pltpu.make_async_remote_copy(
            src_ref=src,
            dst_ref=piece_of(p, q),
            send_sem=w_send.at[kind, p],
            recv_sem=w_recv.at[p, q],
            device_id=target,
        )

    def wait_piece(p, q):
        pltpu.make_async_remote_copy(
            src_ref=piece_of(p, q),
            dst_ref=piece_of(p, q),
            send_sem=w_send.at[0, 0],
            recv_sem=w_recv.at[p, q],
            device_id={"fsdp": f, "dp": core_peer},
        ).wait_recv()

    own_piece = weight_ref.at[:, rows_of(d, piece)]

    @pl.when(can_up)
    def _():
        piece_copy(own_piece, f, d, 0, up).start()

    @pl.when(can_down)
    def _():
        piece_copy(own_piece, f, d, 1, down).start()

    piece_copy(own_piece, f, d, 2, to_y).start()

    def each_side(step, base, body):
        if step == 0:
            body(base, None)
            return

        @pl.when(zi >= step)
        def _():
            body((base + n_fsdp - 2 * step) % n_fsdp, True)

        @pl.when(zi + step < n_z)
        def _():
            body((base + 2 * step) % n_fsdp, False)

    def spread(p):
        piece_copy(piece_of(p, d), p, d, 3, to_x).start()
        piece_copy(piece_of(p, d), p, d, 4, to_core).start()

    def forward_z(step):
        def body(p, rising):
            wait_piece(p, d)
            src = piece_of(p, d)

            @pl.when(can_up if rising else can_down)
            def _():
                piece_copy(src, p, d, 0 if rising else 1, up if rising else down).start()

            piece_copy(src, p, d, 2, to_y).start()
            spread(p)

        each_side(step, f, body)

    def forward_y(step):
        def body(p, rising):
            wait_piece(p, d)
            spread(p)

        each_side(step, y_peer, body)

    def forward_x(step):
        def body(p, rising):
            wait_piece(p, x_peer)
            piece_copy(piece_of(p, x_peer), p, x_peer, 5, to_core).start()

        if step > 0:
            each_side(step, f, body)
        each_side(step, y_peer, body)

    def finish_pieces():
        def moved(p, rising):
            piece_copy(piece_of(p, d), p, d, 2, to_y).wait_send()

            @pl.when(can_up if rising else can_down)
            def _():
                piece_copy(piece_of(p, d), p, d, 0 if rising else 1, up if rising else down).wait_send()

        for step in range(1, n_z):
            each_side(step, f, moved)

        @pl.when(can_up)
        def _():
            piece_copy(own_piece, f, d, 0, up).wait_send()

        @pl.when(can_down)
        def _():
            piece_copy(own_piece, f, d, 1, down).wait_send()

        piece_copy(own_piece, f, d, 2, to_y).wait_send()
        for k in range(1, n_fsdp):
            p = (f + k) % n_fsdp
            piece_copy(piece_of(p, d), p, d, 3, to_x).wait_send()
            piece_copy(piece_of(p, d), p, d, 4, to_core).wait_send()
            piece_copy(piece_of(p, x_peer), p, x_peer, 5, to_core).wait_send()

    def exchange(src, dst, send_sem, recv_sem):
        copies = []
        for k in range(1, n_fsdp):
            target = (f + k) % n_fsdp
            copy = pltpu.make_async_remote_copy(
                src_ref=src.at[rows_of(target, slots)],
                dst_ref=dst.at[rows_of(f, slots)],
                send_sem=send_sem.at[target],
                recv_sem=recv_sem.at[f],
                device_id={"fsdp": target, "dp": d},
            )
            copy.start()
            copies.append(copy)
        dst[rows_of(f, slots), :] = src[rows_of(f, slots), :]
        return copies

    def finish_exchange(copies, src, dst, send_sem, recv_sem):
        for k in range(1, n_fsdp):
            source = (f + k) % n_fsdp
            pltpu.make_async_remote_copy(
                src_ref=src.at[rows_of(source, slots)],
                dst_ref=dst.at[rows_of(source, slots)],
                send_sem=send_sem.at[source],
                recv_sem=recv_sem.at[source],
                device_id={"fsdp": source, "dp": d},
            ).wait_recv()
        pending.extend(copies)

    park = (
        lax.broadcasted_iota(jnp.int32, (rows, owned), 0) == owner_ref[...]
    ).astype(F32).astype(BF16)
    parked[...] = jnp.dot(park, cot_ref[...], preferred_element_type=F32).astype(BF16)

    w_buf[rows_of(f, panel), :] = weight_ref[...]

    ends = []
    total = jnp.int32(0)
    for u in range(utts):
        total = total + counts_ref[0, u]
        ends.append(total)
    pos = lax.broadcasted_iota(jnp.int32, (rows, LANES), 0)

    def segment(at):
        seg = jnp.zeros((rows, LANES), jnp.int32)
        for end in ends:
            seg = seg + (at >= end).astype(jnp.int32)
        return seg

    own_seg = segment(pos)
    live = pos < total
    live_f = live.astype(F32)
    masks = []
    for j in range(taps):
        at = pos + (j - half)
        same = (segment(at) == own_seg) & live & (at >= 0) & (at < rows)
        masks.append(same.astype(F32))

    def lanes_of(i):
        return pl.ds(pl.multiple_of(i * LANES, LANES), LANES)

    def shifted(x, offset):
        return x if offset == 0 else pltpu.roll(x, (-offset) % rows, 0)

    def conv_step(i, acc):
        a = glu_ref[:, lanes_of(i)].astype(F32)
        b = glu_ref[:, pl.ds(pl.multiple_of(chans + i * LANES, LANES), LANES)].astype(F32)
        mixed = a * sigmoid(b) * live_f
        mixed_buf[:, lanes_of(i)] = mixed
        conv = jnp.zeros((rows, LANES), F32)
        for j in range(taps):
            conv = conv + masks[j] * shifted(mixed, j - half) * taps_ref[j : j + 1, lanes_of(i)]
        conv_buf[:, lanes_of(i)] = conv
        return acc + conv

    zero_acc = jnp.zeros((rows, LANES), F32)
    acc = lax.fori_loop(0, n_chunks // 2, conv_step, zero_acc)
    forward_z(1)
    forward_y(0)
    acc = lax.fori_loop(n_chunks // 2, n_chunks, conv_step, acc)
    mean = jnp.sum(acc, axis=1, keepdims=True) * (1.0 / chans)

    forward_z(2)
    forward_y(1)
    cot_copies = exchange(parked, returned, cot_send, cot_recv)

    def var_step(i, acc):
        diff = conv_buf[:, lanes_of(i)] - mean
        return acc + diff * diff

    acc = lax.fori_loop(0, n_chunks, var_step, zero_acc)
    rstd = lax.rsqrt(jnp.sum(acc, axis=1, keepdims=True) * (1.0 / chans) + eps)

    for step in range(3, n_z):
        forward_z(step)
    forward_y(2)

    def act_step(i, carry):
        xhat = (conv_buf[:, lanes_of(i)] - mean) * rstd
        conv_buf[:, lanes_of(i)] = xhat
        normed = xhat * gain_ref[lanes_of(i)][None, :] + bias_ref[lanes_of(i)][None, :]
        acts[:, lanes_of(i)] = (normed * sigmoid(normed) * live_f).astype(BF16)
        return carry

    lax.fori_loop(0, n_chunks, act_step, 0)
    pick = (
        lax.broadcasted_iota(jnp.int32, (rows, rows), 0) == send_ref[...]
    ).astype(F32).astype(BF16)
    outgoing[...] = lax.dot_general(
        pick, acts[...], (((0,), (0,)), ((), ())), preferred_element_type=F32
    ).astype(BF16)

    for step in range(3, n_z):
        forward_y(step)
    for step in range(n_z):
        forward_x(step)

    finish_exchange(cot_copies, parked, returned, cot_send, cot_recv)
    act_copies = exchange(outgoing, arrived, act_send, act_recv)
    home[...] = jnp.dot(pick, returned[...], preferred_element_type=F32).astype(BF16)

    wide = 2 * LANES

    def back_part(step):
        def wait_core(p):
            wait_piece(p, core_peer)
            wait_piece(p, (core_peer + n_dp // 2) % n_dp)

        def body(p, rising):
            wait_core(p + 1 - 2 * (p % 2))
            if step > 0:
                wait_core(p)
            at = rows_of(p // 2, 2 * panel)
            back_buf[:, at] = lax.dot_general(
                home[...], w_buf[at, :], (((1,), (1,)), ((), ())), preferred_element_type=F32
            ).astype(BF16)

        each_side(step, f, body)

    for step in range(n_z):
        back_part(step)

    part = dp_in.at[d]
    dp_in[d] = jnp.zeros(dp_in.shape[1:], F32)

    def norm_step(i, sums):
        xhat = conv_buf[:, lanes_of(i)]
        gain = gain_ref[lanes_of(i)][None, :]
        normed = xhat * gain + bias_ref[lanes_of(i)][None, :]
        s = sigmoid(normed)
        g = back_buf[:, lanes_of(i)].astype(F32) * live_f
        dn = g * (s + normed * s * (1.0 - s))
        dnx = dn * xhat
        part[taps : taps + 1, lanes_of(i)] = jnp.sum(dnx, axis=0, keepdims=True)
        part[taps + 1 : taps + 2, lanes_of(i)] = jnp.sum(dn, axis=0, keepdims=True)
        grad_buf[:, lanes_of(i)] = dn * gain
        return sums[0] + dn * gain, sums[1] + dnx * gain

    first, second = lax.fori_loop(0, n_chunks, norm_step, (zero_acc, zero_acc))
    first = jnp.sum(first, axis=1, keepdims=True) * (1.0 / chans)
    second = jnp.sum(second, axis=1, keepdims=True) * (1.0 / chans)

    def grad_step(i, carry):
        dconv = rstd * (grad_buf[:, lanes_of(i)] - first - conv_buf[:, lanes_of(i)] * second)
        mixed = mixed_buf[:, lanes_of(i)]
        dmixed = jnp.zeros((rows, LANES), F32)
        for j in range(taps):
            moved = masks[taps - 1 - j] * shifted(dconv, half - j)
            part[j : j + 1, lanes_of(i)] = jnp.sum(mixed * moved, axis=0, keepdims=True)
            dmixed = dmixed + moved * taps_ref[j : j + 1, lanes_of(i)]
        grad_buf[:, lanes_of(i)] = dmixed
        return carry

    lax.fori_loop(0, n_chunks, grad_step, 0)

    dp_copies = []
    for k in range(1, n_dp):
        target = (d + k) % n_dp
        copy = pltpu.make_async_remote_copy(
            src_ref=dp_in.at[d],
            dst_ref=dp_in.at[d],
            send_sem=dp_send.at[k],
            recv_sem=dp_recv.at[d],
            device_id={"fsdp": f, "dp": target},
        )
        copy.start()
        dp_copies.append(copy)

    def input_step(i, carry):
        a = glu_ref[:, lanes_of(i)].astype(F32)
        right = pl.ds(pl.multiple_of(chans + i * LANES, LANES), LANES)
        sb = sigmoid(glu_ref[:, right].astype(F32))
        ds = grad_buf[:, lanes_of(i)] * sb
        igrad_ref[:, lanes_of(i)] = ds.astype(BF16)
        igrad_ref[:, right] = (ds * a * (1.0 - sb)).astype(BF16)
        return carry

    lax.fori_loop(0, n_chunks, input_step, 0)

    for k in range(1, n_dp):
        source = (d + k) % n_dp
        pltpu.make_async_remote_copy(
            src_ref=dp_in.at[source],
            dst_ref=dp_in.at[source],
            send_sem=dp_send.at[k],
            recv_sem=dp_recv.at[source],
            device_id={"fsdp": f, "dp": source},
        ).wait_recv()
    pending.extend(dp_copies)
    summed = dp_in[0]
    for q in range(1, n_dp):
        summed = summed + dp_in[q]
    rs_src[...] = summed

    rs_copies = []
    for k in range(1, n_fsdp):
        target = (f + k) % n_fsdp
        copy = pltpu.make_async_remote_copy(
            src_ref=rs_src.at[:, rows_of(target, chunk)],
            dst_ref=rs_in.at[f],
            send_sem=rs_send.at[target],
            recv_sem=rs_recv.at[f],
            device_id={"fsdp": target, "dp": d},
        )
        copy.start()
        rs_copies.append(copy)
    rs_in[f] = rs_src[:, rows_of(f, chunk)]

    finish_exchange(act_copies, outgoing, arrived, act_send, act_recv)
    outgoing_rows = lax.dot_general(
        park, arrived[...], (((0,), (0,)), ((), ())), preferred_element_type=F32
    ).astype(BF16)
    acts[0:owned, :] = outgoing_rows

    def out_step(i, carry):
        at = pl.ds(pl.multiple_of(i * wide, wide), wide)
        out_ref[:, at] = jnp.dot(
            acts[0:owned, :], w_buf[:, at], preferred_element_type=F32
        ).astype(BF16)
        return carry

    lax.fori_loop(0, cols // wide, out_step, 0)

    for k in range(1, n_fsdp):
        source = (f + k) % n_fsdp
        pltpu.make_async_remote_copy(
            src_ref=rs_src.at[:, rows_of(source, chunk)],
            dst_ref=rs_in.at[source],
            send_sem=rs_send.at[source],
            recv_sem=rs_recv.at[source],
            device_id={"fsdp": source, "dp": d},
        ).wait_recv()
    pending.extend(rs_copies)
    reduced = rs_in[0]
    for q in range(1, n_fsdp):
        reduced = reduced + rs_in[q]
    scale = 1.0 / math.sqrt(owned * n_fsdp * n_dp)
    full[:, rows_of(f, chunk)] = reduced * scale
    ag_copies = []
    for k in range(1, n_fsdp):
        target = (f + k) % n_fsdp
        copy = pltpu.make_async_remote_copy(
            src_ref=full.at[:, rows_of(f, chunk)],
            dst_ref=full.at[:, rows_of(f, chunk)],
            send_sem=ag_send.at[target],
            recv_sem=ag_recv.at[f],
            device_id={"fsdp": target, "dp": d},
        )
        copy.start()
        ag_copies.append(copy)
    for k in range(1, n_fsdp):
        source = (f + k) % n_fsdp
        pltpu.make_async_remote_copy(
            src_ref=full.at[:, rows_of(source, chunk)],
            dst_ref=full.at[:, rows_of(source, chunk)],
            send_sem=ag_send.at[source],
            recv_sem=ag_recv.at[source],
            device_id={"fsdp": source, "dp": d},
        ).wait_recv()
    pending.extend(ag_copies)
    kgrad_ref[...] = full[0:taps, 0:chans]
    ngrad_ref[...] = full[taps : taps + 2, 0:chans]
    finish_pieces()
    for copy in pending:
        copy.wait_send()


def fused_call(
    n_fsdp,
    n_dp,
    glu_input,
    frame_counts,
    send_rows,
    owner_rows,
    depth_kernel,
    norm_gain,
    norm_bias,
    point_weight,
    cotangent,
):
    rows, glu_cols = glu_input.shape
    taps, chans = depth_kernel.shape
    panel, cols = point_weight.shape
    owned = cotangent.shape[0]
    sum_rows = -(-(taps + 2) // 8) * 8
    chunk = -(-chans // (n_fsdp * LANES)) * LANES
    padded = chunk * n_fsdp
    vmem = pl.BlockSpec(memory_space=pltpu.VMEM)
    smem = pl.BlockSpec(memory_space=pltpu.SMEM)
    dma = pltpu.SemaphoreType.DMA
    results = pl.pallas_call(
        functools.partial(fused_kernel, n_fsdp, n_dp),
        out_shape=(
            jax.ShapeDtypeStruct((owned, cols), BF16),
            jax.ShapeDtypeStruct((rows, glu_cols), BF16),
            jax.ShapeDtypeStruct((taps, chans), F32),
            jax.ShapeDtypeStruct((2, chans), F32),
        ),
        in_specs=[smem] + [vmem] * 8,
        out_specs=(vmem,) * 4,
        scratch_shapes=[
            pltpu.VMEM((chans, cols), BF16),
            pltpu.VMEM((rows, cols), BF16),
            pltpu.VMEM((rows, cols), BF16),
            pltpu.VMEM((rows, cols), BF16),
            pltpu.VMEM((rows, chans), BF16),
            pltpu.VMEM((rows, chans), BF16),
            pltpu.VMEM((rows, chans), BF16),
            pltpu.VMEM((rows, chans), F32),
            pltpu.VMEM((rows, chans), F32),
            pltpu.VMEM((rows, chans), F32),
            pltpu.VMEM((rows, chans), BF16),
            pltpu.VMEM((n_dp, sum_rows, padded), F32),
            pltpu.VMEM((sum_rows, padded), F32),
            pltpu.VMEM((n_fsdp, sum_rows, chunk), F32),
            pltpu.VMEM((sum_rows, padded), F32),
            dma((6, n_fsdp)),
            dma((n_fsdp, n_dp)),
            dma((n_fsdp,)),
            dma((n_fsdp,)),
            dma((n_fsdp,)),
            dma((n_fsdp,)),
            dma((n_dp,)),
            dma((n_dp,)),
            dma((n_fsdp,)),
            dma((n_fsdp,)),
            dma((n_fsdp,)),
            dma((n_fsdp,)),
        ],
        compiler_params=pltpu.CompilerParams(
            collective_id=0, has_side_effects=True, vmem_limit_bytes=56 * 1024 * 1024
        ),
        name="fused_module",
    )(
        frame_counts,
        glu_input,
        send_rows,
        owner_rows,
        depth_kernel,
        norm_gain,
        norm_bias,
        point_weight,
        cotangent,
    )
    anywhere = pl.BlockSpec(memory_space=pl.ANY)
    return tuple(
        pl.pallas_call(
            copy_kernel,
            out_shape=tuple(jax.ShapeDtypeStruct(r.shape, r.dtype) for r in results),
            in_specs=[anywhere] * 4,
            out_specs=(anywhere,) * 4,
            scratch_shapes=[pltpu.VMEM(r.shape, r.dtype) for r in results]
            + [dma((4, COPY_PARTS))] * 2,
            compiler_params=pltpu.CompilerParams(vmem_limit_bytes=60 * 1024 * 1024),
            name="copy_results",
        )(*results)
    )


def conv_module(glu_rows, counts, kernel, gain_vec, bias_vec):
    row_count = glu_rows.shape[0]
    chan_count = kernel.shape[1]
    half_width = kernel.shape[0] // 2
    values = glu_rows.astype(jnp.float32)
    mixed_vals = values[:, :chan_count] * jax.nn.sigmoid(values[:, chan_count:])
    utter_ends = jnp.cumsum(counts)
    position = jnp.arange(row_count, dtype=jnp.int32)
    segment = jnp.sum((position[:, None] >= utter_ends[None, :]).astype(jnp.int32), axis=1)
    is_live = position < utter_ends[-1]
    mixed_vals = jnp.where(is_live[:, None], mixed_vals, 0.0)
    padded = jnp.pad(mixed_vals, ((half_width, half_width), (0, 0)))
    labels = jnp.pad(segment, (half_width, half_width), constant_values=-1)
    conv_out = jnp.zeros((row_count, chan_count), jnp.float32)
    for offset in range(2 * half_width + 1):
        same_utt = labels[offset : offset + row_count] == segment
        conv_out = (
            conv_out
            + jnp.where(same_utt[:, None], padded[offset : offset + row_count], 0.0)
            * kernel[offset]
        )
    center = jnp.mean(conv_out, axis=1, keepdims=True)
    spread = jnp.mean(jnp.square(conv_out - center), axis=1, keepdims=True)
    normed = (conv_out - center) * lax.rsqrt(spread + eps) * gain_vec + bias_vec
    activated = normed * jax.nn.sigmoid(normed)
    return jnp.where(is_live[:, None], activated, 0.0)


def per_device(
    glu_input,
    frame_counts,
    send_rows,
    owner_rows,
    depth_kernel,
    norm_gain,
    norm_bias,
    point_weight,
    cotangent,
):
    counts = frame_counts[0]
    send_slot = send_rows[0]
    owner_slot = owner_rows[0]
    row_count = glu_input.shape[0]
    out_count = point_weight.shape[1]

    def local_pass(glu_rows, kernel, gain_vec, bias_vec):
        return conv_module(glu_rows, counts, kernel, gain_vec, bias_vec)

    activated, pullback = jax.vjp(local_pass, glu_input, depth_kernel, norm_gain, norm_bias)
    activations = activated.astype(jnp.bfloat16)
    produced = jnp.dot(
        activations,
        lax.all_gather(point_weight, "fsdp", axis=0, tiled=True),
        preferred_element_type=jnp.float32,
    ).astype(jnp.bfloat16)
    outgoing = jnp.concatenate([produced, jnp.zeros((1, out_count), jnp.bfloat16)], axis=0)[
        send_slot
    ]
    arrived = lax.all_to_all(outgoing, "fsdp", split_axis=0, concat_axis=0, tiled=True)
    output = arrived[owner_slot]
    parked = jnp.zeros((row_count, out_count), jnp.bfloat16).at[owner_slot].set(cotangent)
    returned = lax.all_to_all(parked, "fsdp", split_axis=0, concat_axis=0, tiled=True)
    home_rows = (
        jnp.zeros((row_count + 1, out_count), jnp.bfloat16).at[send_slot].set(returned)[:row_count]
    )
    grad_acts = lax.dot_general(
        home_rows,
        lax.all_gather(point_weight, "fsdp", axis=0, tiled=True),
        (((1,), (1,)), ((), ())),
        preferred_element_type=jnp.float32,
    ).astype(jnp.bfloat16)
    input_grad, kernel_part, gain_part, bias_part = pullback(grad_acts.astype(jnp.float32))
    totals = lax.psum((kernel_part, jnp.stack([gain_part, bias_part])), ("fsdp", "dp"))
    frame_total = owner_slot.shape[0] * lax.axis_size("fsdp") * lax.axis_size("dp")
    grad_scale = 1.0 / math.sqrt(frame_total)
    return (output, input_grad, totals[0] * grad_scale, totals[1] * grad_scale)


def solution(mesh):
    in_specs = (
        P(("fsdp", "dp"), None),
        P(("fsdp", "dp"), None),
        P(("fsdp", "dp"), None),
        P(("fsdp", "dp"), None),
        P(),
        P(),
        P(),
        P("fsdp", None),
        P(("fsdp", "dp"), None),
    )
    out_specs = (P(("fsdp", "dp"), None), P(("fsdp", "dp"), None), P(), P())
    n_fsdp, n_dp = mesh.shape["fsdp"], mesh.shape["dp"]

    def local(*args):
        slots = args[2].shape[1] // n_fsdp
        panel = args[7].shape[0]
        if slots % 16 == 0 and panel % 16 == 0 and n_fsdp % 2 == 0 and n_fsdp >= 6 and n_dp == 4 and panel % 64 == 0:
            return fused_call(n_fsdp, n_dp, *args)
        return per_device(*args)

    return jax.shard_map(
        local, mesh=mesh, in_specs=in_specs, out_specs=out_specs, check_vma=False
    )
```

```python
import functools
import math

import jax
import jax.numpy as jnp
from jax import lax
from jax.experimental import pallas as pl
from jax.experimental.pallas import tpu as pltpu
from jax.sharding import PartitionSpec as P

eps = 1e-05
LANES = 128
COPY_PARTS = 2
F32 = jnp.float32
BF16 = jnp.bfloat16


def sigmoid(x):
    return 0.5 * jnp.tanh(0.5 * x) + 0.5


def copy_kernel(*refs):
    sources, targets, stages, in_sems, out_sems = refs[:4], refs[4:8], refs[8:12], refs[12], refs[13]
    loads, stores = [], []
    for i, (source, target, stage) in enumerate(zip(sources, targets, stages)):
        size = source.shape[0]
        parts = COPY_PARTS if size % (16 * COPY_PARTS) == 0 else 1
        step = size // parts
        for k in range(parts):
            at = pl.ds(k * step, step)
            src, mid, dst = (r if parts == 1 else r.at[at] for r in (source, stage, target))
            loads.append(pltpu.make_async_copy(src, mid, in_sems.at[i, k]))
            stores.append(pltpu.make_async_copy(mid, dst, out_sems.at[i, k]))
    for load in loads:
        load.start()
    for load, store in zip(loads, stores):
        load.wait()
        store.start()
    for store in stores:
        store.wait()


def fused_kernel(
    n_fsdp,
    n_dp,
    counts_ref,
    glu_hbm,
    send_ref,
    owner_ref,
    taps_ref,
    gain_ref,
    bias_ref,
    weight_ref,
    cot_hbm,
    out_ref,
    igrad_hbm,
    kgrad_ref,
    ngrad_ref,
    glu_ref,
    cot_ref,
    igrad_ref,
    shift_buf,
    io_sems,
    w_buf,
    parked,
    returned,
    home,
    acts,
    outgoing,
    arrived,
    mixed_buf,
    conv_buf,
    grad_buf,
    back_buf,
    dp_in,
    rs_src,
    rs_in,
    full,
    w_send,
    w_recv,
    cot_send,
    cot_recv,
    act_send,
    act_recv,
    dp_send,
    dp_recv,
    rs_send,
    rs_recv,
    ag_send,
    ag_recv,
):
    f = lax.axis_index("fsdp")
    d = lax.axis_index("dp")
    rows = glu_ref.shape[0]
    chans = taps_ref.shape[1]
    taps = taps_ref.shape[0]
    half = taps // 2
    panel = weight_ref.shape[0]
    cols = weight_ref.shape[1]
    piece = cols // n_dp
    slots = rows // n_fsdp
    owned = cot_ref.shape[0]
    utts = counts_ref.shape[1]
    chunk = full.shape[1] // n_fsdp
    n_chunks = chans // LANES

    y_peer = f + 1 - 2 * (f % 2)
    x_peer = (d + n_dp // 2) % n_dp
    core_peer = d + 1 - 2 * (d % 2)

    panel_rows = pl.ds(pl.multiple_of(f * panel, panel), panel)
    cot_load = pltpu.make_async_copy(cot_hbm, cot_ref, io_sems.at[0])
    glu_load = pltpu.make_async_copy(glu_hbm, glu_ref, io_sems.at[1])
    panel_load = pltpu.make_async_copy(weight_ref, w_buf.at[panel_rows], io_sems.at[2])
    cot_load.start()
    glu_load.start()
    panel_load.start()
    shift_buf[...] = jnp.zeros_like(shift_buf)

    barrier = pltpu.get_barrier_semaphore()
    for k in range(1, n_fsdp):
        pl.semaphore_signal(barrier, inc=1, device_id={"fsdp": (f + k) % n_fsdp, "dp": d})
    for k in range(1, n_dp):
        pl.semaphore_signal(barrier, inc=1, device_id={"fsdp": f, "dp": (d + k) % n_dp})
    pl.semaphore_wait(barrier, n_fsdp + n_dp - 2)

    def rows_of(p, size):
        return pl.ds(pl.multiple_of(p * size, size), size)

    def piece_of(p, q):
        return w_buf.at[rows_of(p, panel), rows_of(q, piece)]

    pending = []
    zi = f // 2
    n_z = n_fsdp // 2
    up, down = {"fsdp": (f + 2) % n_fsdp, "dp": d}, {"fsdp": (f + n_fsdp - 2) % n_fsdp, "dp": d}
    to_y, to_x, to_core = (
        {"fsdp": y_peer, "dp": d},
        {"fsdp": f, "dp": x_peer},
        {"fsdp": f, "dp": core_peer},
    )
    can_up, can_down = zi + 1 < n_z, zi >= 1

    def piece_copy(src, p, q, kind, target):
        return pltpu.make_async_remote_copy(
            src_ref=src,
            dst_ref=piece_of(p, q),
            send_sem=w_send.at[kind, p],
            recv_sem=w_recv.at[p, q],
            device_id=target,
        )

    def wait_piece(p, q):
        pltpu.make_async_remote_copy(
            src_ref=piece_of(p, q),
            dst_ref=piece_of(p, q),
            send_sem=w_send.at[0, 0],
            recv_sem=w_recv.at[p, q],
            device_id={"fsdp": f, "dp": core_peer},
        ).wait_recv()

    own_piece = weight_ref.at[:, rows_of(d, piece)]

    @pl.when(can_up)
    def _():
        piece_copy(own_piece, f, d, 0, up).start()

    @pl.when(can_down)
    def _():
        piece_copy(own_piece, f, d, 1, down).start()

    piece_copy(own_piece, f, d, 2, to_y).start()

    def each_side(step, base, body):
        if step == 0:
            body(base, None)
            return

        @pl.when(zi >= step)
        def _():
            body((base + n_fsdp - 2 * step) % n_fsdp, True)

        @pl.when(zi + step < n_z)
        def _():
            body((base + 2 * step) % n_fsdp, False)

    def spread(p):
        piece_copy(piece_of(p, d), p, d, 3, to_x).start()
        piece_copy(piece_of(p, d), p, d, 4, to_core).start()

    def forward_z(step):
        def body(p, rising):
            wait_piece(p, d)
            src = piece_of(p, d)

            @pl.when(can_up if rising else can_down)
            def _():
                piece_copy(src, p, d, 0 if rising else 1, up if rising else down).start()

            piece_copy(src, p, d, 2, to_y).start()
            spread(p)

        each_side(step, f, body)

    def forward_y(step):
        def body(p, rising):
            wait_piece(p, d)
            spread(p)

        each_side(step, y_peer, body)

    def forward_x(step):
        def body(p, rising):
            wait_piece(p, x_peer)
            piece_copy(piece_of(p, x_peer), p, x_peer, 5, to_core).start()

        if step > 0:
            each_side(step, f, body)
        each_side(step, y_peer, body)

    def finish_pieces():
        def moved(p, rising):
            piece_copy(piece_of(p, d), p, d, 2, to_y).wait_send()

            @pl.when(can_up if rising else can_down)
            def _():
                piece_copy(piece_of(p, d), p, d, 0 if rising else 1, up if rising else down).wait_send()

        for step in range(1, n_z):
            each_side(step, f, moved)

        @pl.when(can_up)
        def _():
            piece_copy(own_piece, f, d, 0, up).wait_send()

        @pl.when(can_down)
        def _():
            piece_copy(own_piece, f, d, 1, down).wait_send()

        piece_copy(own_piece, f, d, 2, to_y).wait_send()
        for k in range(1, n_fsdp):
            p = (f + k) % n_fsdp
            piece_copy(piece_of(p, d), p, d, 3, to_x).wait_send()
            piece_copy(piece_of(p, d), p, d, 4, to_core).wait_send()
            piece_copy(piece_of(p, x_peer), p, x_peer, 5, to_core).wait_send()

    def exchange(src, dst, send_sem, recv_sem):
        copies = []
        for k in range(1, n_fsdp):
            target = (f + k) % n_fsdp
            copy = pltpu.make_async_remote_copy(
                src_ref=src.at[rows_of(target, slots)],
                dst_ref=dst.at[rows_of(f, slots)],
                send_sem=send_sem.at[target],
                recv_sem=recv_sem.at[f],
                device_id={"fsdp": target, "dp": d},
            )
            copy.start()
            copies.append(copy)
        dst[rows_of(f, slots), :] = src[rows_of(f, slots), :]
        return copies

    def finish_exchange(copies, src, dst, send_sem, recv_sem):
        for k in range(1, n_fsdp):
            source = (f + k) % n_fsdp
            pltpu.make_async_remote_copy(
                src_ref=src.at[rows_of(source, slots)],
                dst_ref=dst.at[rows_of(source, slots)],
                send_sem=send_sem.at[source],
                recv_sem=recv_sem.at[source],
                device_id={"fsdp": source, "dp": d},
            ).wait_recv()
        pending.extend(copies)

    park = (
        lax.broadcasted_iota(jnp.int32, (rows, owned), 0) == owner_ref[...]
    ).astype(F32).astype(BF16)
    cot_load.wait()
    parked[...] = jnp.dot(park, cot_ref[...], preferred_element_type=F32).astype(BF16)

    glu_load.wait()
    panel_load.wait()

    ends = []
    total = jnp.int32(0)
    for u in range(utts):
        total = total + counts_ref[0, u]
        ends.append(total)
    pos = lax.broadcasted_iota(jnp.int32, (rows, LANES), 0)

    def segment(at):
        seg = jnp.zeros((rows, LANES), jnp.int32)
        for end in ends:
            seg = seg + (at >= end).astype(jnp.int32)
        return seg

    own_seg = segment(pos)
    live = pos < total
    live_f = live.astype(F32)
    masks = []
    for j in range(taps):
        at = pos + (j - half)
        same = (segment(at) == own_seg) & live & (at >= 0) & (at < rows)
        masks.append(same.astype(F32))

    def lanes_of(i):
        return pl.ds(pl.multiple_of(i * LANES, LANES), LANES)

    def shifted(x, mask, offset):
        if offset == 0:
            return x
        return mask * shift_buf[8 + offset : 8 + offset + rows, :]

    def conv_step(i, acc):
        a = glu_ref[:, lanes_of(i)].astype(F32)
        b = glu_ref[:, pl.ds(pl.multiple_of(chans + i * LANES, LANES), LANES)].astype(F32)
        mixed = a * sigmoid(b) * live_f
        mixed_buf[:, lanes_of(i)] = mixed
        shift_buf[8 : 8 + rows, :] = mixed
        conv = jnp.zeros((rows, LANES), F32)
        for j in range(taps):
            conv = conv + shifted(mixed, masks[j], j - half) * taps_ref[j : j + 1, lanes_of(i)]
        conv_buf[:, lanes_of(i)] = conv
        return acc + conv

    zero_acc = jnp.zeros((rows, LANES), F32)
    acc = lax.fori_loop(0, n_chunks // 2, conv_step, zero_acc)
    forward_z(1)
    forward_y(0)
    acc = lax.fori_loop(n_chunks // 2, n_chunks, conv_step, acc)
    mean = jnp.sum(acc, axis=1, keepdims=True) * (1.0 / chans)

    forward_z(2)
    forward_y(1)
    cot_copies = exchange(parked, returned, cot_send, cot_recv)

    def var_step(i, acc):
        diff = conv_buf[:, lanes_of(i)] - mean
        return acc + diff * diff

    acc = lax.fori_loop(0, n_chunks, var_step, zero_acc)
    rstd = lax.rsqrt(jnp.sum(acc, axis=1, keepdims=True) * (1.0 / chans) + eps)

    for step in range(3, n_z):
        forward_z(step)
    forward_y(2)

    def act_step(i, carry):
        xhat = (conv_buf[:, lanes_of(i)] - mean) * rstd
        conv_buf[:, lanes_of(i)] = xhat
        normed = xhat * gain_ref[lanes_of(i)][None, :] + bias_ref[lanes_of(i)][None, :]
        acts[:, lanes_of(i)] = (normed * sigmoid(normed) * live_f).astype(BF16)
        return carry

    lax.fori_loop(0, n_chunks, act_step, 0)
    pick = (
        lax.broadcasted_iota(jnp.int32, (rows, rows), 0) == send_ref[...]
    ).astype(F32).astype(BF16)
    outgoing[...] = lax.dot_general(
        pick, acts[...], (((0,), (0,)), ((), ())), preferred_element_type=F32
    ).astype(BF16)

    for step in range(3, n_z):
        forward_y(step)
    forward_x(0)
    forward_x(1)
    act_copies = exchange(outgoing, arrived, act_send, act_recv)
    for step in range(2, n_z):
        forward_x(step)

    finish_exchange(cot_copies, parked, returned, cot_send, cot_recv)
    home[...] = jnp.dot(pick, returned[...], preferred_element_type=F32).astype(BF16)

    wide = 2 * LANES

    def back_part(step):
        def wait_core(p):
            wait_piece(p, core_peer)
            wait_piece(p, (core_peer + n_dp // 2) % n_dp)

        def body(p, rising):
            wait_core(p + 1 - 2 * (p % 2))
            if step > 0:
                wait_core(p)
            at = rows_of(p // 2, 2 * panel)
            back_buf[:, at] = lax.dot_general(
                home[...], w_buf[at, :], (((1,), (1,)), ((), ())), preferred_element_type=F32
            ).astype(BF16)

        each_side(step, f, body)

    for step in range(n_z):
        back_part(step)

    part = dp_in.at[d]
    dp_in[d] = jnp.zeros(dp_in.shape[1:], F32)

    def norm_step(i, sums):
        xhat = conv_buf[:, lanes_of(i)]
        gain = gain_ref[lanes_of(i)][None, :]
        normed = xhat * gain + bias_ref[lanes_of(i)][None, :]
        s = sigmoid(normed)
        g = back_buf[:, lanes_of(i)].astype(F32) * live_f
        dn = g * (s + normed * s * (1.0 - s))
        dnx = dn * xhat
        part[taps : taps + 1, lanes_of(i)] = jnp.sum(dnx, axis=0, keepdims=True)
        part[taps + 1 : taps + 2, lanes_of(i)] = jnp.sum(dn, axis=0, keepdims=True)
        grad_buf[:, lanes_of(i)] = dn * gain
        return sums[0] + dn * gain, sums[1] + dnx * gain

    first, second = lax.fori_loop(0, n_chunks, norm_step, (zero_acc, zero_acc))
    first = jnp.sum(first, axis=1, keepdims=True) * (1.0 / chans)
    second = jnp.sum(second, axis=1, keepdims=True) * (1.0 / chans)

    def grad_step(i, carry):
        dconv = rstd * (grad_buf[:, lanes_of(i)] - first - conv_buf[:, lanes_of(i)] * second)
        shift_buf[8 : 8 + rows, :] = dconv
        mixed = mixed_buf[:, lanes_of(i)]
        dmixed = jnp.zeros((rows, LANES), F32)
        for j in range(taps):
            moved = shifted(dconv, masks[taps - 1 - j], half - j)
            part[j : j + 1, lanes_of(i)] = jnp.sum(mixed * moved, axis=0, keepdims=True)
            dmixed = dmixed + moved * taps_ref[j : j + 1, lanes_of(i)]
        grad_buf[:, lanes_of(i)] = dmixed
        return carry

    lax.fori_loop(0, n_chunks, grad_step, 0)

    dp_copies = []
    for k in range(1, n_dp):
        target = (d + k) % n_dp
        copy = pltpu.make_async_remote_copy(
            src_ref=dp_in.at[d],
            dst_ref=dp_in.at[d],
            send_sem=dp_send.at[k],
            recv_sem=dp_recv.at[d],
            device_id={"fsdp": f, "dp": target},
        )
        copy.start()
        dp_copies.append(copy)

    def input_step(i, carry):
        a = glu_ref[:, lanes_of(i)].astype(F32)
        right = pl.ds(pl.multiple_of(chans + i * LANES, LANES), LANES)
        sb = sigmoid(glu_ref[:, right].astype(F32))
        ds = grad_buf[:, lanes_of(i)] * sb
        igrad_ref[:, lanes_of(i)] = ds.astype(BF16)
        igrad_ref[:, right] = (ds * a * (1.0 - sb)).astype(BF16)
        return carry

    lax.fori_loop(0, n_chunks // 2, input_step, 0)

    for k in range(1, n_dp):
        source = (d + k) % n_dp
        pltpu.make_async_remote_copy(
            src_ref=dp_in.at[source],
            dst_ref=dp_in.at[source],
            send_sem=dp_send.at[k],
            recv_sem=dp_recv.at[source],
            device_id={"fsdp": f, "dp": source},
        ).wait_recv()
    pending.extend(dp_copies)
    summed = dp_in[0]
    for q in range(1, n_dp):
        summed = summed + dp_in[q]
    rs_src[...] = summed

    rs_copies = []
    for k in range(1, n_fsdp):
        target = (f + k) % n_fsdp
        copy = pltpu.make_async_remote_copy(
            src_ref=rs_src.at[:, rows_of(target, chunk)],
            dst_ref=rs_in.at[f],
            send_sem=rs_send.at[target],
            recv_sem=rs_recv.at[f],
            device_id={"fsdp": target, "dp": d},
        )
        copy.start()
        rs_copies.append(copy)
    rs_in[f] = rs_src[:, rows_of(f, chunk)]

    lax.fori_loop(n_chunks // 2, n_chunks, input_step, 0)
    igrad_store = pltpu.make_async_copy(igrad_ref, igrad_hbm, io_sems.at[3])
    igrad_store.start()

    for k in range(1, n_fsdp):
        source = (f + k) % n_fsdp
        pltpu.make_async_remote_copy(
            src_ref=rs_src.at[:, rows_of(source, chunk)],
            dst_ref=rs_in.at[source],
            send_sem=rs_send.at[source],
            recv_sem=rs_recv.at[source],
            device_id={"fsdp": source, "dp": d},
        ).wait_recv()
    pending.extend(rs_copies)
    reduced = rs_in[0]
    for q in range(1, n_fsdp):
        reduced = reduced + rs_in[q]
    scale = 1.0 / math.sqrt(owned * n_fsdp * n_dp)
    full[:, rows_of(f, chunk)] = reduced * scale
    ag_copies = []
    for k in range(1, n_fsdp):
        target = (f + k) % n_fsdp
        copy = pltpu.make_async_remote_copy(
            src_ref=full.at[:, rows_of(f, chunk)],
            dst_ref=full.at[:, rows_of(f, chunk)],
            send_sem=ag_send.at[target],
            recv_sem=ag_recv.at[f],
            device_id={"fsdp": target, "dp": d},
        )
        copy.start()
        ag_copies.append(copy)

    finish_exchange(act_copies, outgoing, arrived, act_send, act_recv)
    outgoing_rows = lax.dot_general(
        park, arrived[...], (((0,), (0,)), ((), ())), preferred_element_type=F32
    ).astype(BF16)
    acts[0:owned, :] = outgoing_rows

    def out_step(i, carry):
        at = pl.ds(pl.multiple_of(i * wide, wide), wide)
        out_ref[:, at] = jnp.dot(
            acts[0:owned, :], w_buf[:, at], preferred_element_type=F32
        ).astype(BF16)
        return carry

    lax.fori_loop(0, cols // wide, out_step, 0)

    for k in range(1, n_fsdp):
        source = (f + k) % n_fsdp
        pltpu.make_async_remote_copy(
            src_ref=full.at[:, rows_of(source, chunk)],
            dst_ref=full.at[:, rows_of(source, chunk)],
            send_sem=ag_send.at[source],
            recv_sem=ag_recv.at[source],
            device_id={"fsdp": source, "dp": d},
        ).wait_recv()
    pending.extend(ag_copies)
    kgrad_ref[...] = full[0:taps, 0:chans]
    ngrad_ref[...] = full[taps : taps + 2, 0:chans]
    igrad_store.wait()
    finish_pieces()
    for copy in pending:
        copy.wait_send()


def fused_call(
    n_fsdp,
    n_dp,
    glu_input,
    frame_counts,
    send_rows,
    owner_rows,
    depth_kernel,
    norm_gain,
    norm_bias,
    point_weight,
    cotangent,
):
    rows, glu_cols = glu_input.shape
    taps, chans = depth_kernel.shape
    panel, cols = point_weight.shape
    owned = cotangent.shape[0]
    sum_rows = -(-(taps + 2) // 8) * 8
    chunk = -(-chans // (n_fsdp * LANES)) * LANES
    padded = chunk * n_fsdp
    vmem = pl.BlockSpec(memory_space=pltpu.VMEM)
    anywhere = pl.BlockSpec(memory_space=pl.ANY)
    smem = pl.BlockSpec(memory_space=pltpu.SMEM)
    dma = pltpu.SemaphoreType.DMA
    results = pl.pallas_call(
        functools.partial(fused_kernel, n_fsdp, n_dp),
        out_shape=(
            jax.ShapeDtypeStruct((owned, cols), BF16),
            jax.ShapeDtypeStruct((rows, glu_cols), BF16),
            jax.ShapeDtypeStruct((taps, chans), F32),
            jax.ShapeDtypeStruct((2, chans), F32),
        ),
        in_specs=[smem, anywhere] + [vmem] * 5 + [anywhere] * 2,
        out_specs=(vmem, anywhere, vmem, vmem),
        scratch_shapes=[
            pltpu.VMEM((rows, glu_cols), BF16),
            pltpu.VMEM((owned, cols), BF16),
            pltpu.VMEM((rows, glu_cols), BF16),
            pltpu.VMEM((rows + 16, LANES), F32),
            dma((4,)),
            pltpu.VMEM((chans, cols), BF16),
            pltpu.VMEM((rows, cols), BF16),
            pltpu.VMEM((rows, cols), BF16),
            pltpu.VMEM((rows, cols), BF16),
            pltpu.VMEM((rows, chans), BF16),
            pltpu.VMEM((rows, chans), BF16),
            pltpu.VMEM((rows, chans), BF16),
            pltpu.VMEM((rows, chans), F32),
            pltpu.VMEM((rows, chans), F32),
            pltpu.VMEM((rows, chans), F32),
            pltpu.VMEM((rows, chans), BF16),
            pltpu.VMEM((n_dp, sum_rows, padded), F32),
            pltpu.VMEM((sum_rows, padded), F32),
            pltpu.VMEM((n_fsdp, sum_rows, chunk), F32),
            pltpu.VMEM((sum_rows, padded), F32),
            dma((6, n_fsdp)),
            dma((n_fsdp, n_dp)),
            dma((n_fsdp,)),
            dma((n_fsdp,)),
            dma((n_fsdp,)),
            dma((n_fsdp,)),
            dma((n_dp,)),
            dma((n_dp,)),
            dma((n_fsdp,)),
            dma((n_fsdp,)),
            dma((n_fsdp,)),
            dma((n_fsdp,)),
        ],
        compiler_params=pltpu.CompilerParams(
            collective_id=0, has_side_effects=True, vmem_limit_bytes=56 * 1024 * 1024
        ),
        name="fused_module",
    )(
        frame_counts,
        glu_input,
        send_rows,
        owner_rows,
        depth_kernel,
        norm_gain,
        norm_bias,
        point_weight,
        cotangent,
    )
    return tuple(
        pl.pallas_call(
            copy_kernel,
            out_shape=tuple(jax.ShapeDtypeStruct(r.shape, r.dtype) for r in results),
            in_specs=[anywhere] * 4,
            out_specs=(anywhere,) * 4,
            scratch_shapes=[pltpu.VMEM(r.shape, r.dtype) for r in results]
            + [dma((4, COPY_PARTS))] * 2,
            compiler_params=pltpu.CompilerParams(vmem_limit_bytes=60 * 1024 * 1024),
            name="copy_results",
        )(*results)
    )


def conv_module(glu_rows, counts, kernel, gain_vec, bias_vec):
    row_count = glu_rows.shape[0]
    chan_count = kernel.shape[1]
    half_width = kernel.shape[0] // 2
    values = glu_rows.astype(jnp.float32)
    mixed_vals = values[:, :chan_count] * jax.nn.sigmoid(values[:, chan_count:])
    utter_ends = jnp.cumsum(counts)
    position = jnp.arange(row_count, dtype=jnp.int32)
    segment = jnp.sum((position[:, None] >= utter_ends[None, :]).astype(jnp.int32), axis=1)
    is_live = position < utter_ends[-1]
    mixed_vals = jnp.where(is_live[:, None], mixed_vals, 0.0)
    padded = jnp.pad(mixed_vals, ((half_width, half_width), (0, 0)))
    labels = jnp.pad(segment, (half_width, half_width), constant_values=-1)
    conv_out = jnp.zeros((row_count, chan_count), jnp.float32)
    for offset in range(2 * half_width + 1):
        same_utt = labels[offset : offset + row_count] == segment
        conv_out = (
            conv_out
            + jnp.where(same_utt[:, None], padded[offset : offset + row_count], 0.0)
            * kernel[offset]
        )
    center = jnp.mean(conv_out, axis=1, keepdims=True)
    spread = jnp.mean(jnp.square(conv_out - center), axis=1, keepdims=True)
    normed = (conv_out - center) * lax.rsqrt(spread + eps) * gain_vec + bias_vec
    activated = normed * jax.nn.sigmoid(normed)
    return jnp.where(is_live[:, None], activated, 0.0)


def per_device(
    glu_input,
    frame_counts,
    send_rows,
    owner_rows,
    depth_kernel,
    norm_gain,
    norm_bias,
    point_weight,
    cotangent,
):
    counts = frame_counts[0]
    send_slot = send_rows[0]
    owner_slot = owner_rows[0]
    row_count = glu_input.shape[0]
    out_count = point_weight.shape[1]

    def local_pass(glu_rows, kernel, gain_vec, bias_vec):
        return conv_module(glu_rows, counts, kernel, gain_vec, bias_vec)

    activated, pullback = jax.vjp(local_pass, glu_input, depth_kernel, norm_gain, norm_bias)
    activations = activated.astype(jnp.bfloat16)
    produced = jnp.dot(
        activations,
        lax.all_gather(point_weight, "fsdp", axis=0, tiled=True),
        preferred_element_type=jnp.float32,
    ).astype(jnp.bfloat16)
    outgoing = jnp.concatenate([produced, jnp.zeros((1, out_count), jnp.bfloat16)], axis=0)[
        send_slot
    ]
    arrived = lax.all_to_all(outgoing, "fsdp", split_axis=0, concat_axis=0, tiled=True)
    output = arrived[owner_slot]
    parked = jnp.zeros((row_count, out_count), jnp.bfloat16).at[owner_slot].set(cotangent)
    returned = lax.all_to_all(parked, "fsdp", split_axis=0, concat_axis=0, tiled=True)
    home_rows = (
        jnp.zeros((row_count + 1, out_count), jnp.bfloat16).at[send_slot].set(returned)[:row_count]
    )
    grad_acts = lax.dot_general(
        home_rows,
        lax.all_gather(point_weight, "fsdp", axis=0, tiled=True),
        (((1,), (1,)), ((), ())),
        preferred_element_type=jnp.float32,
    ).astype(jnp.bfloat16)
    input_grad, kernel_part, gain_part, bias_part = pullback(grad_acts.astype(jnp.float32))
    totals = lax.psum((kernel_part, jnp.stack([gain_part, bias_part])), ("fsdp", "dp"))
    frame_total = owner_slot.shape[0] * lax.axis_size("fsdp") * lax.axis_size("dp")
    grad_scale = 1.0 / math.sqrt(frame_total)
    return (output, input_grad, totals[0] * grad_scale, totals[1] * grad_scale)


def solution(mesh):
    in_specs = (
        P(("fsdp", "dp"), None),
        P(("fsdp", "dp"), None),
        P(("fsdp", "dp"), None),
        P(("fsdp", "dp"), None),
        P(),
        P(),
        P(),
        P("fsdp", None),
        P(("fsdp", "dp"), None),
    )
    out_specs = (P(("fsdp", "dp"), None), P(("fsdp", "dp"), None), P(), P())
    n_fsdp, n_dp = mesh.shape["fsdp"], mesh.shape["dp"]

    def local(*args):
        slots = args[2].shape[1] // n_fsdp
        panel = args[7].shape[0]
        if slots % 16 == 0 and panel % 16 == 0 and n_fsdp % 2 == 0 and n_fsdp >= 6 and n_dp == 4 and panel % 64 == 0:
            return fused_call(n_fsdp, n_dp, *args)
        return per_device(*args)

    return jax.shard_map(
        local, mesh=mesh, in_specs=in_specs, out_specs=out_specs, check_vma=False
    )
```

```python
import functools
import math

import jax
import jax.numpy as jnp
from jax import lax
from jax.experimental import pallas as pl
from jax.experimental.pallas import tpu as pltpu
from jax.sharding import PartitionSpec as P

eps = 1e-05
LANES = 128
COPY_PARTS = 2
F32 = jnp.float32
BF16 = jnp.bfloat16


def sigmoid(x):
    return 0.5 * jnp.tanh(0.5 * x) + 0.5


def copy_kernel(*refs):
    sources, targets, stages, in_sems, out_sems = refs[:4], refs[4:8], refs[8:12], refs[12], refs[13]
    loads, stores = [], []
    for i, (source, target, stage) in enumerate(zip(sources, targets, stages)):
        size = source.shape[0]
        parts = COPY_PARTS if size % (16 * COPY_PARTS) == 0 else 1
        step = size // parts
        for k in range(parts):
            at = pl.ds(k * step, step)
            src, mid, dst = (r if parts == 1 else r.at[at] for r in (source, stage, target))
            loads.append(pltpu.make_async_copy(src, mid, in_sems.at[i, k]))
            stores.append(pltpu.make_async_copy(mid, dst, out_sems.at[i, k]))
    for load in loads:
        load.start()
    for load, store in zip(loads, stores):
        load.wait()
        store.start()
    for store in stores:
        store.wait()


def fused_kernel(
    n_fsdp,
    n_dp,
    counts_ref,
    glu_hbm,
    send_ref,
    owner_ref,
    taps_ref,
    gain_ref,
    bias_ref,
    weight_ref,
    cot_hbm,
    out_ref,
    igrad_hbm,
    kgrad_ref,
    ngrad_ref,
    glu_ref,
    cot_ref,
    igrad_ref,
    shift_buf,
    io_sems,
    w_buf,
    parked,
    returned,
    home,
    acts,
    outgoing,
    arrived,
    mixed_buf,
    conv_buf,
    grad_buf,
    back_buf,
    dp_in,
    rs_src,
    rs_in,
    full,
    w_send,
    w_recv,
    cot_send,
    cot_recv,
    act_send,
    act_recv,
    dp_send,
    dp_recv,
    rs_send,
    rs_recv,
    ag_send,
    ag_recv,
):
    f = lax.axis_index("fsdp")
    d = lax.axis_index("dp")
    rows = glu_ref.shape[0]
    chans = taps_ref.shape[1]
    taps = taps_ref.shape[0]
    half = taps // 2
    panel = weight_ref.shape[0]
    cols = weight_ref.shape[1]
    piece = cols // n_dp
    slots = rows // n_fsdp
    owned = cot_ref.shape[0]
    utts = counts_ref.shape[1]
    chunk = full.shape[1] // n_fsdp
    n_chunks = chans // LANES

    y_peer = f + 1 - 2 * (f % 2)
    x_peer = (d + n_dp // 2) % n_dp
    core_peer = d + 1 - 2 * (d % 2)

    panel_rows = pl.ds(pl.multiple_of(f * panel, panel), panel)
    cot_load = pltpu.make_async_copy(cot_hbm, cot_ref, io_sems.at[0])
    glu_load = pltpu.make_async_copy(glu_hbm, glu_ref, io_sems.at[1])
    panel_load = pltpu.make_async_copy(weight_ref, w_buf.at[panel_rows], io_sems.at[2])
    cot_load.start()
    glu_load.start()
    panel_load.start()
    shift_buf[...] = jnp.zeros_like(shift_buf)

    barrier = pltpu.get_barrier_semaphore()
    for k in range(1, n_fsdp):
        pl.semaphore_signal(barrier, inc=1, device_id={"fsdp": (f + k) % n_fsdp, "dp": d})
    for k in range(1, n_dp):
        pl.semaphore_signal(barrier, inc=1, device_id={"fsdp": f, "dp": (d + k) % n_dp})
    pl.semaphore_wait(barrier, n_fsdp + n_dp - 2)

    def rows_of(p, size):
        return pl.ds(pl.multiple_of(p * size, size), size)

    def piece_of(p, q):
        return w_buf.at[rows_of(p, panel), rows_of(q, piece)]

    pending = []
    zi = f // 2
    n_z = n_fsdp // 2
    up, down = {"fsdp": (f + 2) % n_fsdp, "dp": d}, {"fsdp": (f + n_fsdp - 2) % n_fsdp, "dp": d}
    to_y, to_x, to_core = (
        {"fsdp": y_peer, "dp": d},
        {"fsdp": f, "dp": x_peer},
        {"fsdp": f, "dp": core_peer},
    )
    can_up, can_down = zi + 1 < n_z, zi >= 1

    def piece_copy(src, p, q, kind, target):
        return pltpu.make_async_remote_copy(
            src_ref=src,
            dst_ref=piece_of(p, q),
            send_sem=w_send.at[kind, p],
            recv_sem=w_recv.at[p, q],
            device_id=target,
        )

    def wait_piece(p, q):
        pltpu.make_async_remote_copy(
            src_ref=piece_of(p, q),
            dst_ref=piece_of(p, q),
            send_sem=w_send.at[0, 0],
            recv_sem=w_recv.at[p, q],
            device_id={"fsdp": f, "dp": core_peer},
        ).wait_recv()

    own_piece = weight_ref.at[:, rows_of(d, piece)]

    @pl.when(can_up)
    def _():
        piece_copy(own_piece, f, d, 0, up).start()

    @pl.when(can_down)
    def _():
        piece_copy(own_piece, f, d, 1, down).start()

    piece_copy(own_piece, f, d, 2, to_y).start()

    def each_side(step, base, body):
        if step == 0:
            body(base, None)
            return

        @pl.when(zi >= step)
        def _():
            body((base + n_fsdp - 2 * step) % n_fsdp, True)

        @pl.when(zi + step < n_z)
        def _():
            body((base + 2 * step) % n_fsdp, False)

    def spread(p):
        piece_copy(piece_of(p, d), p, d, 3, to_x).start()
        piece_copy(piece_of(p, d), p, d, 4, to_core).start()

    def forward_z(step):
        def body(p, rising):
            wait_piece(p, d)
            src = piece_of(p, d)

            @pl.when(can_up if rising else can_down)
            def _():
                piece_copy(src, p, d, 0 if rising else 1, up if rising else down).start()

            piece_copy(src, p, d, 2, to_y).start()
            spread(p)

        each_side(step, f, body)

    def forward_y(step):
        def body(p, rising):
            wait_piece(p, d)
            spread(p)

        each_side(step, y_peer, body)

    def forward_x(step):
        def body(p, rising):
            wait_piece(p, x_peer)
            piece_copy(piece_of(p, x_peer), p, x_peer, 5, to_core).start()

        if step > 0:
            each_side(step, f, body)
        each_side(step, y_peer, body)

    def finish_pieces():
        def moved(p, rising):
            piece_copy(piece_of(p, d), p, d, 2, to_y).wait_send()

            @pl.when(can_up if rising else can_down)
            def _():
                piece_copy(piece_of(p, d), p, d, 0 if rising else 1, up if rising else down).wait_send()

        for step in range(1, n_z):
            each_side(step, f, moved)

        @pl.when(can_up)
        def _():
            piece_copy(own_piece, f, d, 0, up).wait_send()

        @pl.when(can_down)
        def _():
            piece_copy(own_piece, f, d, 1, down).wait_send()

        piece_copy(own_piece, f, d, 2, to_y).wait_send()
        for k in range(1, n_fsdp):
            p = (f + k) % n_fsdp
            piece_copy(piece_of(p, d), p, d, 3, to_x).wait_send()
            piece_copy(piece_of(p, d), p, d, 4, to_core).wait_send()
            piece_copy(piece_of(p, x_peer), p, x_peer, 5, to_core).wait_send()

    def exchange(src, dst, send_sem, recv_sem):
        copies = []
        for k in range(1, n_fsdp):
            target = (f + k) % n_fsdp
            copy = pltpu.make_async_remote_copy(
                src_ref=src.at[rows_of(target, slots)],
                dst_ref=dst.at[rows_of(f, slots)],
                send_sem=send_sem.at[target],
                recv_sem=recv_sem.at[f],
                device_id={"fsdp": target, "dp": d},
            )
            copy.start()
            copies.append(copy)
        dst[rows_of(f, slots), :] = src[rows_of(f, slots), :]
        return copies

    def finish_exchange(copies, src, dst, send_sem, recv_sem):
        for k in range(1, n_fsdp):
            source = (f + k) % n_fsdp
            pltpu.make_async_remote_copy(
                src_ref=src.at[rows_of(source, slots)],
                dst_ref=dst.at[rows_of(source, slots)],
                send_sem=send_sem.at[source],
                recv_sem=recv_sem.at[source],
                device_id={"fsdp": source, "dp": d},
            ).wait_recv()
        pending.extend(copies)

    park = (
        lax.broadcasted_iota(jnp.int32, (rows, owned), 0) == owner_ref[...]
    ).astype(F32).astype(BF16)
    cot_load.wait()
    parked[...] = jnp.dot(park, cot_ref[...], preferred_element_type=F32).astype(BF16)

    glu_load.wait()
    panel_load.wait()

    ends = []
    total = jnp.int32(0)
    for u in range(utts):
        total = total + counts_ref[0, u]
        ends.append(total)
    pos = lax.broadcasted_iota(jnp.int32, (rows, LANES), 0)

    def segment(at):
        seg = jnp.zeros((rows, LANES), jnp.int32)
        for end in ends:
            seg = seg + (at >= end).astype(jnp.int32)
        return seg

    own_seg = segment(pos)
    live = pos < total
    live_f = live.astype(F32)
    masks = []
    for j in range(taps):
        at = pos + (j - half)
        same = (segment(at) == own_seg) & live & (at >= 0) & (at < rows)
        masks.append(same.astype(F32))

    def lanes_of(i):
        return pl.ds(pl.multiple_of(i * LANES, LANES), LANES)

    def shifted(x, mask, offset):
        if offset == 0:
            return x
        return mask * shift_buf[8 + offset : 8 + offset + rows, :]

    def conv_step(i, acc):
        a = glu_ref[:, lanes_of(i)].astype(F32)
        b = glu_ref[:, pl.ds(pl.multiple_of(chans + i * LANES, LANES), LANES)].astype(F32)
        mixed = a * sigmoid(b) * live_f
        mixed_buf[:, lanes_of(i)] = mixed
        shift_buf[8 : 8 + rows, :] = mixed
        conv = jnp.zeros((rows, LANES), F32)
        for j in range(taps):
            conv = conv + shifted(mixed, masks[j], j - half) * taps_ref[j : j + 1, lanes_of(i)]
        conv_buf[:, lanes_of(i)] = conv
        return acc + conv

    zero_acc = jnp.zeros((rows, LANES), F32)
    acc = lax.fori_loop(0, n_chunks // 2, conv_step, zero_acc)
    forward_z(1)
    forward_y(0)
    acc = lax.fori_loop(n_chunks // 2, n_chunks, conv_step, acc)
    mean = jnp.sum(acc, axis=1, keepdims=True) * (1.0 / chans)

    forward_z(2)
    forward_y(1)
    cot_copies = exchange(parked, returned, cot_send, cot_recv)

    def var_step(i, acc):
        diff = conv_buf[:, lanes_of(i)] - mean
        return acc + diff * diff

    acc = lax.fori_loop(0, n_chunks, var_step, zero_acc)
    rstd = lax.rsqrt(jnp.sum(acc, axis=1, keepdims=True) * (1.0 / chans) + eps)

    for step in range(3, n_z):
        forward_z(step)
    forward_y(2)

    def act_step(i, carry):
        xhat = (conv_buf[:, lanes_of(i)] - mean) * rstd
        conv_buf[:, lanes_of(i)] = xhat
        normed = xhat * gain_ref[lanes_of(i)][None, :] + bias_ref[lanes_of(i)][None, :]
        acts[:, lanes_of(i)] = (normed * sigmoid(normed) * live_f).astype(BF16)
        return carry

    lax.fori_loop(0, n_chunks, act_step, 0)
    pick = (
        lax.broadcasted_iota(jnp.int32, (rows, rows), 0) == send_ref[...]
    ).astype(F32).astype(BF16)
    outgoing[...] = lax.dot_general(
        pick, acts[...], (((0,), (0,)), ((), ())), preferred_element_type=F32
    ).astype(BF16)

    for step in range(3, n_z):
        forward_y(step)
    for step in range(n_z):
        forward_x(step)

    finish_exchange(cot_copies, parked, returned, cot_send, cot_recv)
    act_copies = exchange(outgoing, arrived, act_send, act_recv)
    home[...] = jnp.dot(pick, returned[...], preferred_element_type=F32).astype(BF16)

    wide = 2 * LANES

    def back_part(step):
        def wait_core(p):
            wait_piece(p, core_peer)
            wait_piece(p, (core_peer + n_dp // 2) % n_dp)

        def body(p, rising):
            wait_core(p + 1 - 2 * (p % 2))
            if step > 0:
                wait_core(p)
            at = rows_of(p // 2, 2 * panel)
            back_buf[:, at] = lax.dot_general(
                home[...], w_buf[at, :], (((1,), (1,)), ((), ())), preferred_element_type=F32
            ).astype(BF16)

        each_side(step, f, body)

    for step in range(n_z):
        back_part(step)

    part = dp_in.at[d]
    dp_in[d] = jnp.zeros(dp_in.shape[1:], F32)

    def norm_step(i, sums):
        xhat = conv_buf[:, lanes_of(i)]
        gain = gain_ref[lanes_of(i)][None, :]
        normed = xhat * gain + bias_ref[lanes_of(i)][None, :]
        s = sigmoid(normed)
        g = back_buf[:, lanes_of(i)].astype(F32) * live_f
        dn = g * (s + normed * s * (1.0 - s))
        dnx = dn * xhat
        part[taps : taps + 1, lanes_of(i)] = jnp.sum(dnx, axis=0, keepdims=True)
        part[taps + 1 : taps + 2, lanes_of(i)] = jnp.sum(dn, axis=0, keepdims=True)
        grad_buf[:, lanes_of(i)] = dn * gain
        return sums[0] + dn * gain, sums[1] + dnx * gain

    first, second = lax.fori_loop(0, n_chunks, norm_step, (zero_acc, zero_acc))
    first = jnp.sum(first, axis=1, keepdims=True) * (1.0 / chans)
    second = jnp.sum(second, axis=1, keepdims=True) * (1.0 / chans)

    def grad_step(i, carry):
        dconv = rstd * (grad_buf[:, lanes_of(i)] - first - conv_buf[:, lanes_of(i)] * second)
        shift_buf[8 : 8 + rows, :] = dconv
        mixed = mixed_buf[:, lanes_of(i)]
        dmixed = jnp.zeros((rows, LANES), F32)
        for j in range(taps):
            moved = shifted(dconv, masks[taps - 1 - j], half - j)
            part[j : j + 1, lanes_of(i)] = jnp.sum(mixed * moved, axis=0, keepdims=True)
            dmixed = dmixed + moved * taps_ref[j : j + 1, lanes_of(i)]
        grad_buf[:, lanes_of(i)] = dmixed
        return carry

    lax.fori_loop(0, n_chunks, grad_step, 0)

    dp_copies = []
    for k in range(1, n_dp):
        target = (d + k) % n_dp
        copy = pltpu.make_async_remote_copy(
            src_ref=dp_in.at[d],
            dst_ref=dp_in.at[d],
            send_sem=dp_send.at[k],
            recv_sem=dp_recv.at[d],
            device_id={"fsdp": f, "dp": target},
        )
        copy.start()
        dp_copies.append(copy)

    def input_step(i, carry):
        a = glu_ref[:, lanes_of(i)].astype(F32)
        right = pl.ds(pl.multiple_of(chans + i * LANES, LANES), LANES)
        sb = sigmoid(glu_ref[:, right].astype(F32))
        ds = grad_buf[:, lanes_of(i)] * sb
        igrad_ref[:, lanes_of(i)] = ds.astype(BF16)
        igrad_ref[:, right] = (ds * a * (1.0 - sb)).astype(BF16)
        return carry

    lax.fori_loop(0, n_chunks // 2, input_step, 0)

    for k in range(1, n_dp):
        source = (d + k) % n_dp
        pltpu.make_async_remote_copy(
            src_ref=dp_in.at[source],
            dst_ref=dp_in.at[source],
            send_sem=dp_send.at[k],
            recv_sem=dp_recv.at[source],
            device_id={"fsdp": f, "dp": source},
        ).wait_recv()
    pending.extend(dp_copies)
    summed = dp_in[0]
    for q in range(1, n_dp):
        summed = summed + dp_in[q]
    rs_src[...] = summed

    rs_copies = []
    for k in range(1, n_fsdp):
        target = (f + k) % n_fsdp
        copy = pltpu.make_async_remote_copy(
            src_ref=rs_src.at[:, rows_of(target, chunk)],
            dst_ref=rs_in.at[f],
            send_sem=rs_send.at[target],
            recv_sem=rs_recv.at[f],
            device_id={"fsdp": target, "dp": d},
        )
        copy.start()
        rs_copies.append(copy)
    rs_in[f] = rs_src[:, rows_of(f, chunk)]

    lax.fori_loop(n_chunks // 2, n_chunks, input_step, 0)
    igrad_store = pltpu.make_async_copy(igrad_ref, igrad_hbm, io_sems.at[3])
    igrad_store.start()

    for k in range(1, n_fsdp):
        source = (f + k) % n_fsdp
        pltpu.make_async_remote_copy(
            src_ref=rs_src.at[:, rows_of(source, chunk)],
            dst_ref=rs_in.at[source],
            send_sem=rs_send.at[source],
            recv_sem=rs_recv.at[source],
            device_id={"fsdp": source, "dp": d},
        ).wait_recv()
    pending.extend(rs_copies)
    reduced = rs_in[0]
    for q in range(1, n_fsdp):
        reduced = reduced + rs_in[q]
    scale = 1.0 / math.sqrt(owned * n_fsdp * n_dp)
    full[:, rows_of(f, chunk)] = reduced * scale
    ag_copies = []
    for k in range(1, n_fsdp):
        target = (f + k) % n_fsdp
        copy = pltpu.make_async_remote_copy(
            src_ref=full.at[:, rows_of(f, chunk)],
            dst_ref=full.at[:, rows_of(f, chunk)],
            send_sem=ag_send.at[target],
            recv_sem=ag_recv.at[f],
            device_id={"fsdp": target, "dp": d},
        )
        copy.start()
        ag_copies.append(copy)

    finish_exchange(act_copies, outgoing, arrived, act_send, act_recv)
    outgoing_rows = lax.dot_general(
        park, arrived[...], (((0,), (0,)), ((), ())), preferred_element_type=F32
    ).astype(BF16)
    acts[0:owned, :] = outgoing_rows

    def out_step(i, carry):
        at = pl.ds(pl.multiple_of(i * wide, wide), wide)
        out_ref[:, at] = jnp.dot(
            acts[0:owned, :], w_buf[:, at], preferred_element_type=F32
        ).astype(BF16)
        return carry

    lax.fori_loop(0, cols // wide, out_step, 0)

    for k in range(1, n_fsdp):
        source = (f + k) % n_fsdp
        pltpu.make_async_remote_copy(
            src_ref=full.at[:, rows_of(source, chunk)],
            dst_ref=full.at[:, rows_of(source, chunk)],
            send_sem=ag_send.at[source],
            recv_sem=ag_recv.at[source],
            device_id={"fsdp": source, "dp": d},
        ).wait_recv()
    pending.extend(ag_copies)
    kgrad_ref[...] = full[0:taps, 0:chans]
    ngrad_ref[...] = full[taps : taps + 2, 0:chans]
    igrad_store.wait()
    finish_pieces()
    for copy in pending:
        copy.wait_send()


def fused_call(
    n_fsdp,
    n_dp,
    glu_input,
    frame_counts,
    send_rows,
    owner_rows,
    depth_kernel,
    norm_gain,
    norm_bias,
    point_weight,
    cotangent,
):
    rows, glu_cols = glu_input.shape
    taps, chans = depth_kernel.shape
    panel, cols = point_weight.shape
    owned = cotangent.shape[0]
    sum_rows = -(-(taps + 2) // 8) * 8
    chunk = -(-chans // (n_fsdp * LANES)) * LANES
    padded = chunk * n_fsdp
    vmem = pl.BlockSpec(memory_space=pltpu.VMEM)
    anywhere = pl.BlockSpec(memory_space=pl.ANY)
    smem = pl.BlockSpec(memory_space=pltpu.SMEM)
    dma = pltpu.SemaphoreType.DMA
    results = pl.pallas_call(
        functools.partial(fused_kernel, n_fsdp, n_dp),
        out_shape=(
            jax.ShapeDtypeStruct((owned, cols), BF16),
            jax.ShapeDtypeStruct((rows, glu_cols), BF16),
            jax.ShapeDtypeStruct((taps, chans), F32),
            jax.ShapeDtypeStruct((2, chans), F32),
        ),
        in_specs=[smem, anywhere] + [vmem] * 5 + [anywhere] * 2,
        out_specs=(vmem, anywhere, vmem, vmem),
        scratch_shapes=[
            pltpu.VMEM((rows, glu_cols), BF16),
            pltpu.VMEM((owned, cols), BF16),
            pltpu.VMEM((rows, glu_cols), BF16),
            pltpu.VMEM((rows + 16, LANES), F32),
            dma((4,)),
            pltpu.VMEM((chans, cols), BF16),
            pltpu.VMEM((rows, cols), BF16),
            pltpu.VMEM((rows, cols), BF16),
            pltpu.VMEM((rows, cols), BF16),
            pltpu.VMEM((rows, chans), BF16),
            pltpu.VMEM((rows, chans), BF16),
            pltpu.VMEM((rows, chans), BF16),
            pltpu.VMEM((rows, chans), F32),
            pltpu.VMEM((rows, chans), F32),
            pltpu.VMEM((rows, chans), F32),
            pltpu.VMEM((rows, chans), BF16),
            pltpu.VMEM((n_dp, sum_rows, padded), F32),
            pltpu.VMEM((sum_rows, padded), F32),
            pltpu.VMEM((n_fsdp, sum_rows, chunk), F32),
            pltpu.VMEM((sum_rows, padded), F32),
            dma((6, n_fsdp)),
            dma((n_fsdp, n_dp)),
            dma((n_fsdp,)),
            dma((n_fsdp,)),
            dma((n_fsdp,)),
            dma((n_fsdp,)),
            dma((n_dp,)),
            dma((n_dp,)),
            dma((n_fsdp,)),
            dma((n_fsdp,)),
            dma((n_fsdp,)),
            dma((n_fsdp,)),
        ],
        compiler_params=pltpu.CompilerParams(
            collective_id=0, has_side_effects=True, vmem_limit_bytes=56 * 1024 * 1024
        ),
        name="fused_module",
    )(
        frame_counts,
        glu_input,
        send_rows,
        owner_rows,
        depth_kernel,
        norm_gain,
        norm_bias,
        point_weight,
        cotangent,
    )
    return tuple(
        pl.pallas_call(
            copy_kernel,
            out_shape=tuple(jax.ShapeDtypeStruct(r.shape, r.dtype) for r in results),
            in_specs=[anywhere] * 4,
            out_specs=(anywhere,) * 4,
            scratch_shapes=[pltpu.VMEM(r.shape, r.dtype) for r in results]
            + [dma((4, COPY_PARTS))] * 2,
            compiler_params=pltpu.CompilerParams(vmem_limit_bytes=60 * 1024 * 1024),
            name="copy_results",
        )(*results)
    )


def conv_module(glu_rows, counts, kernel, gain_vec, bias_vec):
    row_count = glu_rows.shape[0]
    chan_count = kernel.shape[1]
    half_width = kernel.shape[0] // 2
    values = glu_rows.astype(jnp.float32)
    mixed_vals = values[:, :chan_count] * jax.nn.sigmoid(values[:, chan_count:])
    utter_ends = jnp.cumsum(counts)
    position = jnp.arange(row_count, dtype=jnp.int32)
    segment = jnp.sum((position[:, None] >= utter_ends[None, :]).astype(jnp.int32), axis=1)
    is_live = position < utter_ends[-1]
    mixed_vals = jnp.where(is_live[:, None], mixed_vals, 0.0)
    padded = jnp.pad(mixed_vals, ((half_width, half_width), (0, 0)))
    labels = jnp.pad(segment, (half_width, half_width), constant_values=-1)
    conv_out = jnp.zeros((row_count, chan_count), jnp.float32)
    for offset in range(2 * half_width + 1):
        same_utt = labels[offset : offset + row_count] == segment
        conv_out = (
            conv_out
            + jnp.where(same_utt[:, None], padded[offset : offset + row_count], 0.0)
            * kernel[offset]
        )
    center = jnp.mean(conv_out, axis=1, keepdims=True)
    spread = jnp.mean(jnp.square(conv_out - center), axis=1, keepdims=True)
    normed = (conv_out - center) * lax.rsqrt(spread + eps) * gain_vec + bias_vec
    activated = normed * jax.nn.sigmoid(normed)
    return jnp.where(is_live[:, None], activated, 0.0)


def per_device(
    glu_input,
    frame_counts,
    send_rows,
    owner_rows,
    depth_kernel,
    norm_gain,
    norm_bias,
    point_weight,
    cotangent,
):
    counts = frame_counts[0]
    send_slot = send_rows[0]
    owner_slot = owner_rows[0]
    row_count = glu_input.shape[0]
    out_count = point_weight.shape[1]

    def local_pass(glu_rows, kernel, gain_vec, bias_vec):
        return conv_module(glu_rows, counts, kernel, gain_vec, bias_vec)

    activated, pullback = jax.vjp(local_pass, glu_input, depth_kernel, norm_gain, norm_bias)
    activations = activated.astype(jnp.bfloat16)
    produced = jnp.dot(
        activations,
        lax.all_gather(point_weight, "fsdp", axis=0, tiled=True),
        preferred_element_type=jnp.float32,
    ).astype(jnp.bfloat16)
    outgoing = jnp.concatenate([produced, jnp.zeros((1, out_count), jnp.bfloat16)], axis=0)[
        send_slot
    ]
    arrived = lax.all_to_all(outgoing, "fsdp", split_axis=0, concat_axis=0, tiled=True)
    output = arrived[owner_slot]
    parked = jnp.zeros((row_count, out_count), jnp.bfloat16).at[owner_slot].set(cotangent)
    returned = lax.all_to_all(parked, "fsdp", split_axis=0, concat_axis=0, tiled=True)
    home_rows = (
        jnp.zeros((row_count + 1, out_count), jnp.bfloat16).at[send_slot].set(returned)[:row_count]
    )
    grad_acts = lax.dot_general(
        home_rows,
        lax.all_gather(point_weight, "fsdp", axis=0, tiled=True),
        (((1,), (1,)), ((), ())),
        preferred_element_type=jnp.float32,
    ).astype(jnp.bfloat16)
    input_grad, kernel_part, gain_part, bias_part = pullback(grad_acts.astype(jnp.float32))
    totals = lax.psum((kernel_part, jnp.stack([gain_part, bias_part])), ("fsdp", "dp"))
    frame_total = owner_slot.shape[0] * lax.axis_size("fsdp") * lax.axis_size("dp")
    grad_scale = 1.0 / math.sqrt(frame_total)
    return (output, input_grad, totals[0] * grad_scale, totals[1] * grad_scale)


def solution(mesh):
    in_specs = (
        P(("fsdp", "dp"), None),
        P(("fsdp", "dp"), None),
        P(("fsdp", "dp"), None),
        P(("fsdp", "dp"), None),
        P(),
        P(),
        P(),
        P("fsdp", None),
        P(("fsdp", "dp"), None),
    )
    out_specs = (P(("fsdp", "dp"), None), P(("fsdp", "dp"), None), P(), P())
    n_fsdp, n_dp = mesh.shape["fsdp"], mesh.shape["dp"]

    def local(*args):
        slots = args[2].shape[1] // n_fsdp
        panel = args[7].shape[0]
        if slots % 16 == 0 and panel % 16 == 0 and n_fsdp % 2 == 0 and n_fsdp >= 6 and n_dp == 4 and panel % 64 == 0:
            return fused_call(n_fsdp, n_dp, *args)
        return per_device(*args)

    return jax.shard_map(
        local, mesh=mesh, in_specs=in_specs, out_specs=out_specs, check_vma=False
    )
```
